32 devices in a mesh: grp: 4 (over y, x), dev: 8 (over z, core).
Axes of the slice: x: 2, y: 2, z: 4, core: 2. Of those that a mesh axis runs over, the one named last changes fastest.
Arguments:
- node_latent: bfloat16 [4, 2048, 512], P('grp', 'dev'), may hold values from -6 to 6
- edge_latent: bfloat16 [4, 8, 8, 256, 512], P('grp', 'dev'), may hold values from -6 to 6
- node_cotangent: bfloat16 [4, 2048, 512], P('grp', 'dev'), may hold values from -6 to 6
- edge_cotangent: bfloat16 [4, 8, 8, 256, 512], P('grp', 'dev'), may hold values from -6 to 6
- edge_sender: int32 [8, 8, 256], P(None, 'dev'), may hold values from 0 to 255
- edge_receiver: int32 [8, 8, 256], P('dev'), may hold values from 0 to 255
- live_counts: int32 [8, 8], P('dev'), may hold values from 1 to 256, as said below
- edge_lift: bfloat16 [1536, 512], replicated, may hold values from -0.15625 to 0.15625
- edge_bias: float32 [512], replicated, may hold values from -3 to 3
- edge_mix: bfloat16 [512, 512], replicated, may hold values from -0.25 to 0.25
- edge_gain: float32 [512], replicated, may hold values from 0.5 to 2
- node_lift: bfloat16 [1024, 512], replicated, may hold values from -0.1875 to 0.1875
- node_bias: float32 [512], replicated, may hold values from -3 to 3
- node_mix: bfloat16 [512, 512], replicated, may hold values from -0.25 to 0.25
- node_gain: float32 [512], replicated, may hold values from 0.5 to 2
Outputs:
- grad_nodes: float32 [4, 2048, 512], P('grp', 'dev')
- grad_edges: bfloat16 [4, 8, 8, 256, 512], P('grp', 'dev')
- edge_lift_grad: float32 [1536, 512], replicated
- edge_bias_grad: float32 [512], replicated
- edge_mix_grad: float32 [512, 512], replicated
- edge_gain_grad: float32 [512], replicated
- node_lift_grad: float32 [1024, 512], replicated
- node_bias_grad: float32 [512], replicated
- node_mix_grad: float32 [512, 512], replicated
- node_gain_grad: float32 [512], replicated
The draws below stay inside these ranges and needn't reach their ends.
Inputs may be any that keep to these rules, and one draw needn't show every extreme that they name: Slots k >= live_counts[r, s] of block (r, s) are padding. Owners are numbered along a closed curve over the sphere's partition: blocks with r == s or with r and s at most 2 apart around that loop of 8 owners hold most of a receiver's live edges, the other blocks only a few long-range edges; some block of every draw has all 256 slots live.
All inputs are finite; a program needn't handle non-finite values.
Results may differ from the reference program's by a relative error of at most 0.0075.
Values may be sent and summed in bfloat16 or wider, within the bound.
No kernel may reach another device: no remote copies, remote signals or barrier semaphores. Data moves between devices by JAX's collectives and lax.ppermute only.
A program may use at most 128 MiB of HBM per device.

```python
import math
import jax
import jax.numpy as jnp
from jax import lax

D = 512
NODE_DEV = 256
PEERS = 8
SLOT = 256
SAMPLES = 4
NODES = 2048
SLOTS_ALL = 65536
NODES_ALL = 8192


def draw_live_counts(key, part):
    key = jax.random.fold_in(key, 3)
    key_levels, key_fullest, key_near, key_far = jax.random.split(key, 4)
    levels = jax.random.randint(key_levels, (PEERS,), max(1, SLOT // 2), SLOT + 1)
    fullest = jax.random.randint(key_fullest, (), 0, PEERS)
    levels = jnp.where(jnp.arange(PEERS) == fullest, SLOT, levels)
    near_low = jnp.maximum(levels * 3 // 4, 1)
    near_counts = jax.random.randint(key_near, (PEERS, PEERS), near_low[:, None], levels[:, None] + 1)
    far_counts = jax.random.randint(key_far, (PEERS, PEERS), 1, max(2, SLOT // 5 + 1))
    rows = jnp.arange(PEERS)[:, None]
    cols = jnp.arange(PEERS)[None, :]
    apart = jnp.abs(rows - cols)
    distance = jnp.minimum(apart, PEERS - apart)
    counts = jnp.where(distance <= 2, near_counts, far_counts)
    counts = jnp.where(distance == 0, levels[:, None], counts)
    return counts.astype(jnp.int32)


def place_ends(entries, rng, smallest, high):
    extent = entries.shape
    place = [jax.random.randint(jax.random.fold_in(rng, axis), (), 0, extent[axis]) for axis in range(len(extent))]
    entries = entries.at[tuple(place)].set(smallest)
    longest = extent.index(max(extent))
    place[longest] = (place[longest] + 1) % extent[longest]
    return entries.at[tuple(place)].set(high)


def steps_of(rng, extent, cuts, smallest, high):
    loudness = 1.0
    for dim, parts in cuts:
        draws = jax.random.uniform(jax.random.fold_in(jax.random.fold_in(rng, 6), dim), (parts,), jnp.float32, smallest / len(cuts), high / len(cuts))
        loudness = loudness * jnp.repeat(jnp.exp(draws), extent[dim] // parts).reshape((-1,) + (1,) * (len(extent) - 1 - dim))
    return loudness


def noise(stream_key, extent, scale, bound, pieces=(), kind=jnp.bfloat16):
    loudness = steps_of(stream_key, extent, pieces, -0.22, 0.18) if pieces else 1.0
    values = jax.random.normal(stream_key, extent, jnp.float32) * scale * loudness
    return jnp.minimum(jnp.maximum(values, -bound), bound).astype(kind)


def setup_inputs(seed: int = 0) -> dict:
    splits = jax.random.split(jax.random.key(seed), 16)
    return {
        "node_latent": noise(splits[0], (SAMPLES, NODES, D), 1.0, 6.0, ((0, 4), (1, 8))),
        "edge_latent": noise(splits[1], (SAMPLES, PEERS, PEERS, SLOT, D), 1.0, 6.0, ((0, 4), (1, 8))),
        "node_cotangent": noise(splits[2], (SAMPLES, NODES, D), 1.0, 6.0, ((0, 4), (1, 8))),
        "edge_cotangent": noise(splits[3], (SAMPLES, PEERS, PEERS, SLOT, D), 1.0, 6.0, ((0, 4), (1, 8))),
        "edge_sender": place_ends(jax.random.randint(splits[4], (PEERS, PEERS, SLOT), 0, NODE_DEV), jax.random.fold_in(splits[4], 1), 0, NODE_DEV - 1).astype(jnp.int32),
        "edge_receiver": place_ends(jax.random.randint(splits[5], (PEERS, PEERS, SLOT), 0, NODE_DEV), jax.random.fold_in(splits[5], 1), 0, NODE_DEV - 1).astype(jnp.int32),
        "live_counts": draw_live_counts(jax.random.fold_in(splits[15], 71), 0),
        "edge_lift": noise(splits[7], (3 * D, D), (3 * D) ** -0.5, 0.15625),
        "edge_bias": noise(splits[8], (D,), 0.5, 3.0, (), jnp.float32),
        "edge_mix": noise(splits[9], (D, D), D ** -0.5, 0.25),
        "edge_gain": jnp.clip(jnp.exp(jax.random.uniform(splits[10], (D,), jnp.float32, math.log(0.5), math.log(2.0))), 0.5, 2.0),
        "node_lift": noise(splits[11], (2 * D, D), (2 * D) ** -0.5, 0.1875),
        "node_bias": noise(splits[12], (D,), 0.5, 3.0, (), jnp.float32),
        "node_mix": noise(splits[13], (D, D), D ** -0.5, 0.25),
        "node_gain": jnp.clip(jnp.exp(jax.random.uniform(splits[14], (D,), jnp.float32, math.log(0.5), math.log(2.0))), 0.5, 2.0),
    }


EPSILON = 1e-05

def silu_grad(values):
    sigmoid = jax.nn.sigmoid(values)
    return sigmoid * (1.0 + values * (1.0 - sigmoid))

def norm_forward(values):
    centred = values - lax.optimization_barrier(jnp.mean(values, axis=-1, keepdims=True))
    inverse = lax.rsqrt(lax.optimization_barrier(jnp.mean(centred * centred, axis=-1, keepdims=True)) + EPSILON)
    return (centred * inverse, inverse)

def norm_backward(grad_hat, normed, inverse):
    spread = lax.optimization_barrier(jnp.mean(grad_hat * normed, axis=-1, keepdims=True))
    return inverse * (grad_hat - lax.optimization_barrier(jnp.mean(grad_hat, axis=-1, keepdims=True)) - normed * spread)

def matmul(left, right):
    return jnp.dot(left, right, preferred_element_type=jnp.float32)

def reference(node_latent, edge_latent, node_cotangent, edge_cotangent, edge_sender, edge_receiver, live_counts, edge_lift, edge_bias, edge_mix, edge_gain, node_lift, node_bias, node_mix, node_gain):
    width = node_latent.shape[2]
    owners = jnp.arange(PEERS, dtype=jnp.int32)
    sender_global = (owners[None, :, None] * NODE_DEV + edge_sender).reshape(-1).astype(jnp.int32)
    receiver_global = (owners[:, None, None] * NODE_DEV + edge_receiver).reshape(-1).astype(jnp.int32)
    live = (jnp.arange(SLOT, dtype=jnp.int32)[None, None, :] < live_counts[:, :, None]).reshape(-1, 1)
    total_nodes = PEERS * NODE_DEV

    def one_sample(inputs):
        nodes, edges, node_seed, edge_seed = inputs
        edges = edges.reshape(-1, width)
        edge_seed = edge_seed.reshape(-1, width).astype(jnp.float32)
        stacked = jnp.concatenate([edges, nodes[sender_global], nodes[receiver_global]], axis=1)
        pre_edge = matmul(stacked, edge_lift) + edge_bias
        hidden_edge = jax.nn.silu(pre_edge).astype(jnp.bfloat16)
        normed_edge, inverse_edge = norm_forward(matmul(hidden_edge, edge_mix))
        message = jnp.where(live, normed_edge * edge_gain, 0.0).astype(jnp.bfloat16)
        summed = jax.ops.segment_sum(message.astype(jnp.float32), receiver_global, total_nodes).astype(jnp.bfloat16)
        joined = jnp.concatenate([nodes, summed], axis=1)
        pre_node = matmul(joined, node_lift) + node_bias
        hidden_node = jax.nn.silu(pre_node).astype(jnp.bfloat16)
        normed_node, inverse_node = norm_forward(matmul(hidden_node, node_mix))
        grad_update = node_seed.astype(jnp.float32)
        node_gain_grad = lax.optimization_barrier(jnp.sum(grad_update * normed_node, axis=0))
        grad_out_node = norm_backward(grad_update * node_gain, normed_node, inverse_node).astype(jnp.bfloat16)
        node_mix_grad = matmul(hidden_node.T, grad_out_node)
        grad_pre_node = (matmul(grad_out_node, node_mix.T) * silu_grad(pre_node)).astype(jnp.bfloat16)
        node_bias_grad = lax.optimization_barrier(jnp.sum(grad_pre_node.astype(jnp.float32), axis=0))
        node_lift_grad = matmul(joined.T, grad_pre_node)
        grad_joined = matmul(grad_pre_node, node_lift.T)
        grad_message = jnp.where(live, edge_seed + grad_joined[:, width:][receiver_global], 0.0)
        edge_gain_grad = lax.optimization_barrier(jnp.sum(grad_message * normed_edge, axis=0))
        grad_out_edge = norm_backward(grad_message * edge_gain, normed_edge, inverse_edge).astype(jnp.bfloat16)
        edge_mix_grad = matmul(hidden_edge.T, grad_out_edge)
        grad_pre_edge = (matmul(grad_out_edge, edge_mix.T) * silu_grad(pre_edge)).astype(jnp.bfloat16)
        edge_bias_grad = lax.optimization_barrier(jnp.sum(grad_pre_edge.astype(jnp.float32), axis=0))
        edge_lift_grad = matmul(stacked.T, grad_pre_edge)
        grad_rounded = matmul(grad_pre_edge, edge_lift.T).astype(jnp.bfloat16)
        grad_stacked = lax.optimization_barrier(grad_rounded).astype(jnp.float32)
        grad_edges = jnp.where(live, edge_seed + grad_stacked[:, :width], 0.0).astype(jnp.bfloat16)
        from_receivers = jax.ops.segment_sum(grad_stacked[:, 2 * width:], receiver_global, total_nodes)
        from_senders = jax.ops.segment_sum(grad_stacked[:, width:2 * width], sender_global, total_nodes)
        grad_nodes = grad_update + grad_joined[:, :width] + from_receivers + from_senders
        weight_terms = (edge_lift_grad, edge_bias_grad, edge_mix_grad, edge_gain_grad, node_lift_grad, node_bias_grad, node_mix_grad, node_gain_grad)
        return (grad_nodes, grad_edges.reshape(PEERS, PEERS, SLOT, width), weight_terms)
    grad_nodes, grad_edges, weight_terms = lax.map(one_sample, (node_latent, edge_latent, node_cotangent, edge_cotangent))
    totals = jax.tree.map(lambda stacked_terms: lax.optimization_barrier(jnp.sum(stacked_terms, axis=0)), weight_terms)
    edge_scale = float(SLOTS_ALL) ** (-0.5)
    node_scale = float(NODES_ALL) ** (-0.5)
    return (grad_nodes, grad_edges, totals[0] * edge_scale, totals[1] * edge_scale, totals[2] * edge_scale, totals[3] * edge_scale, totals[4] * node_scale, totals[5] * node_scale, totals[6] * node_scale, totals[7] * node_scale)
```

```python
import jax
import jax.numpy as jnp
from jax import lax
from jax.experimental import pallas as pl
from jax.experimental.pallas import tpu as pltpu
from jax.sharding import PartitionSpec as P

EPSILON = 1e-05
CHUNKS = 32
BF16 = jnp.bfloat16
F32 = jnp.float32


def matmul(left, right):
    return jnp.dot(left, right, preferred_element_type=F32)


def contract_rows(left, right):
    return lax.dot_general(left, right, (((0,), (0,)), ((), ())), preferred_element_type=F32)


def contract_features(left, right):
    return lax.dot_general(left, right, (((1,), (1,)), ((), ())), preferred_element_type=F32)


def one_hot(index_row, nodes):
    rows = lax.broadcasted_iota(jnp.int32, (nodes, index_row.shape[1]), 0)
    return jnp.where(rows == index_row, 1.0, 0.0).astype(BF16)


def silu_pair(values):
    gate = 0.5 * jnp.tanh(0.5 * values) + 0.5
    hidden = values * gate
    return hidden, gate + hidden * (1.0 - gate)


def norm_forward(values):
    centred = values - jnp.mean(values, axis=-1, keepdims=True)
    inverse = lax.rsqrt(jnp.mean(centred * centred, axis=-1, keepdims=True) + EPSILON)
    return centred * inverse, inverse


def norm_backward(grad_hat, normed, inverse):
    spread = jnp.mean(grad_hat * normed, axis=-1, keepdims=True)
    return inverse * (grad_hat - jnp.mean(grad_hat, axis=-1, keepdims=True) - normed * spread)


def live_rows(count, shape):
    return lax.broadcasted_iota(jnp.int32, shape, 0) < count


def store_chunks(order_ref, source_ref, target_ref):
    rows = source_ref.shape[0] // CHUNKS

    def step(place, carry):
        start = pl.multiple_of(order_ref[place] * rows, rows)
        target = pl.multiple_of(place * rows, rows)
        target_ref[pl.ds(target, rows), :] = source_ref[pl.ds(start, rows), :].astype(BF16)
        return carry

    lax.fori_loop(0, CHUNKS, step, 0)


def lift_kernel(edges_ref, receiver_ref, nodes_ref, lift_ref, bias_ref, pre_ref):
    width = nodes_ref.shape[1]
    table = one_hot(receiver_ref[0], nodes_ref.shape[0])
    receivers = contract_rows(table, nodes_ref[...]).astype(BF16)
    pre_ref[0] = (
        matmul(edges_ref[0], lift_ref[:width])
        + matmul(receivers, lift_ref[2 * width :])
        + bias_ref[...]
    )


def forward_kernel(
    owner_ref,
    live_ref,
    order_ref,
    pre_ref,
    gathered_ref,
    sender_ref,
    receiver_ref,
    nodes_ref,
    seed_ref,
    lift_ref,
    mix_ref,
    gain_ref,
    node_lift_ref,
    node_bias_ref,
    node_mix_ref,
    node_gain_ref,
    hidden_ref,
    normed_ref,
    slope_ref,
    inverse_ref,
    base_ref,
    summed_grad_ref,
    packed_ref,
    small_ref,
    summed_ref,
    total_ref,
):
    step = pl.program_id(0)
    nodes_count, width = nodes_ref.shape
    owner = owner_ref[step]
    senders = contract_rows(
        one_hot(sender_ref[0], nodes_count), gathered_ref[0, :nodes_count]
    ).astype(BF16)
    pre = pre_ref[0] + matmul(senders, lift_ref[...])
    hidden, slope = silu_pair(pre)
    hidden = hidden.astype(BF16)
    normed, inverse = norm_forward(matmul(hidden, mix_ref[...]))
    hidden_ref[0] = hidden
    slope_ref[0] = slope.astype(BF16)
    normed_ref[0] = normed.astype(BF16)
    inverse_ref[0] = inverse
    live = live_rows(live_ref[owner], normed.shape)
    message = jnp.where(live, normed * gain_ref[...], 0.0).astype(BF16)

    @pl.when(step == 0)
    def _():
        summed_ref[...] = jnp.zeros_like(summed_ref)

    summed_ref[...] += matmul(one_hot(receiver_ref[0], nodes_count), message)

    @pl.when(step == pl.num_programs(0) - 1)
    def _():
        nodes = nodes_ref[...]
        summed = summed_ref[...].astype(BF16)
        pre_node = (
            matmul(nodes, node_lift_ref[:width])
            + matmul(summed, node_lift_ref[width:])
            + node_bias_ref[...]
        )
        hidden_node, slope_node = silu_pair(pre_node)
        hidden_node = hidden_node.astype(BF16)
        normed_node, inverse_node = norm_forward(matmul(hidden_node, node_mix_ref[...]))
        seed = seed_ref[...].astype(F32)
        small_ref[1:2, :] = jnp.sum(seed * normed_node, axis=0, keepdims=True)
        grad_out = norm_backward(seed * node_gain_ref[...], normed_node, inverse_node).astype(BF16)
        total_ref[2 * width :, :] = contract_rows(hidden_node, grad_out)
        grad_pre = (contract_features(grad_out, node_mix_ref[...]) * slope_node).astype(BF16)
        small_ref[0:1, :] = jnp.sum(grad_pre.astype(F32), axis=0, keepdims=True)
        total_ref[:width, :] = contract_rows(nodes, grad_pre)
        total_ref[width : 2 * width, :] = contract_rows(summed, grad_pre)
        base_ref[...] = seed + contract_features(grad_pre, node_lift_ref[:width])
        summed_grad_ref[...] = contract_features(grad_pre, node_lift_ref[width:]).astype(BF16)
        store_chunks(order_ref, total_ref, packed_ref)


def backward_kernel(
    owner_ref,
    live_ref,
    order_ref,
    edges_ref,
    seed_ref,
    gathered_ref,
    sender_ref,
    receiver_ref,
    hidden_ref,
    normed_ref,
    slope_ref,
    inverse_ref,
    nodes_ref,
    base_ref,
    summed_grad_ref,
    lift_ref,
    mix_ref,
    gain_ref,
    grad_edges_ref,
    partial_ref,
    grad_nodes_ref,
    packed_ref,
    small_ref,
    received_ref,
    total_ref,
):
    step = pl.program_id(0)
    nodes_count, width = nodes_ref.shape
    live_count = live_ref[owner_ref[step]]

    @pl.when(step == 0)
    def _():
        received_ref[...] = jnp.zeros_like(received_ref)
        total_ref[...] = jnp.zeros_like(total_ref)
        small_ref[...] = jnp.zeros_like(small_ref)

    seed = seed_ref[0].astype(F32)
    live = live_rows(live_count, seed.shape)
    receiver_table = one_hot(receiver_ref[0], nodes_count)
    grad_message = jnp.where(
        live, seed + contract_rows(receiver_table, summed_grad_ref[...]), 0.0
    )
    normed = normed_ref[0].astype(F32)
    small_ref[1:2, :] += jnp.sum(grad_message * normed, axis=0, keepdims=True)
    grad_out = norm_backward(grad_message * gain_ref[...], normed, inverse_ref[0]).astype(BF16)
    total_ref[3 * width :, :] += contract_rows(hidden_ref[0], grad_out)
    grad_pre = (contract_features(grad_out, mix_ref[...]) * slope_ref[0].astype(F32)).astype(BF16)
    small_ref[0:1, :] += jnp.sum(grad_pre.astype(F32), axis=0, keepdims=True)
    total_ref[:width, :] += contract_rows(edges_ref[0], grad_pre)
    sent = matmul(one_hot(sender_ref[0], nodes_count), grad_pre).astype(BF16)
    partial_ref[0, 0] = sent
    total_ref[width : 2 * width, :] += contract_rows(gathered_ref[0, :nodes_count], sent)
    received_ref[...] += matmul(receiver_table, grad_pre)
    grad_edges_ref[0] = jnp.where(
        live, seed + contract_features(grad_pre, lift_ref[:width]), 0.0
    ).astype(BF16)

    @pl.when(step == pl.num_programs(0) - 1)
    def _():
        received = received_ref[...].astype(BF16)
        total_ref[2 * width : 3 * width, :] = contract_rows(nodes_ref[...], received)
        grad_nodes_ref[...] = base_ref[...] + contract_features(received, lift_ref[2 * width :])
        store_chunks(order_ref, total_ref, packed_ref)


def unpack_kernel(
    scale, order_ref, node_ref, edge_ref, edge_lift_ref, edge_mix_ref, node_lift_ref, node_mix_ref,
    edge_total, node_total,
):
    edge_scale, node_scale = scale
    for source, total, factor in (
        (edge_ref, edge_total, edge_scale),
        (node_ref, node_total, node_scale),
    ):
        rows = source.shape[0] // CHUNKS

        def step(place, carry, source=source, total=total, factor=factor, rows=rows):
            target = pl.multiple_of(order_ref[place] * rows, rows)
            start = pl.multiple_of(place * rows, rows)
            total[pl.ds(target, rows), :] = source[pl.ds(start, rows), :].astype(F32) * factor
            return carry

        lax.fori_loop(0, CHUNKS, step, 0)
    width = edge_lift_ref.shape[1]
    edge_lift_ref[...] = edge_total[: 3 * width]
    edge_mix_ref[...] = edge_total[3 * width :]
    node_lift_ref[...] = node_total[: 2 * width]
    node_mix_ref[...] = node_total[2 * width :]


def swap(values, axis, bit):
    size = lax.axis_size(axis)
    return lax.ppermute(values, axis, [(i, i ^ bit) for i in range(size)])


def add_rounded(left, right):
    return (left.astype(F32) + right.astype(F32)).astype(BF16)


def gather_nodes(nodes):
    pieces = []
    for piece in [nodes] + [swap(nodes, "dev", 2 * k) for k in range(1, 4)]:
        pieces += [piece, swap(piece, "dev", 1)]
    return jnp.stack(pieces)


def reduce_senders(partial):
    kept = add_rounded(partial[0], swap(partial[1], "dev", 1))
    kept = add_rounded(kept[::2], swap(kept[1::2], "dev", 2))
    return kept[0].astype(F32) + swap(kept[1], "dev", 4).astype(F32)


def reduce_plane(packed):
    half = packed.shape[0] // 2
    kept = add_rounded(packed[:half], swap(packed[half:], "dev", 1))
    parts = []
    for side, bits in enumerate(((1, 2), (2, 1))):
        part = kept[side * half // 2 : (side + 1) * half // 2]
        for bit in bits:
            rows = part.shape[0] // 2
            part = add_rounded(part[:rows], swap(part[rows:], "grp", bit))
        parts.append(part)
    return parts


def reduce_line(parts):
    kept_rows = jnp.concatenate([part[: part.shape[0] // 2] for part in parts])
    sent_rows = jnp.concatenate([part[part.shape[0] // 2 :] for part in parts])
    kept = add_rounded(kept_rows, swap(sent_rows, "dev", 2))
    kept = add_rounded(kept, swap(kept, "dev", 4))
    other = swap(kept, "dev", 2)
    results, start = [], 0
    for part in parts:
        rows = part.shape[0] // 2
        results.append(jnp.concatenate([kept[start : start + rows], other[start : start + rows]]))
        start += rows
    return results


def spread_plane(sides):
    for bits in ((2, 1), (1, 2)):
        sides = [
            jnp.concatenate([part, swap(part, "grp", bit)]) for part, bit in zip(sides, bits)
        ]
    return sides


def split_rows(part, sizes):
    pieces, start = [], 0
    for size in sizes:
        pieces.append(part[start : start + size])
        start += size
    return pieces


def chunk_order():
    group = lax.axis_index("grp")
    device = lax.axis_index("dev")
    x, y = group & 1, group >> 1
    core, z = device & 1, (device >> 1) & 1
    place = jnp.arange(CHUNKS, dtype=jnp.int32)
    first = core * 16 + x * 4 + y * 2 + z
    second = core * 16 + y * 4 + x * 2 + z
    return place ^ jnp.where((place & 8) == 0, first, second)


def small_sum(values):
    for axis, bit in (("dev", 1), ("grp", 1), ("grp", 2), ("dev", 2), ("dev", 4)):
        values = values + swap(values, axis, bit)
    return values


def shape(*dims, kind=F32):
    return jax.ShapeDtypeStruct(dims, kind)


def params(mebibytes):
    return pltpu.CompilerParams(vmem_limit_bytes=mebibytes << 20)


def whole(*dims):
    return pl.BlockSpec(dims, lambda *_: (0,) * len(dims))


def per_device(
    node_latent,
    edge_latent,
    node_cotangent,
    edge_cotangent,
    edge_sender,
    edge_receiver,
    live_counts,
    edge_lift,
    edge_bias,
    edge_mix,
    edge_gain,
    node_lift,
    node_bias,
    node_mix,
    node_gain,
):
    width = node_latent.shape[2]
    nodes = node_latent[0]
    count = nodes.shape[0]
    peers = edge_receiver.shape[1]
    slots = edge_receiver.shape[2]
    total_rows = peers * slots
    unit = total_rows * width * width
    edges = edge_latent.reshape(peers, slots, width)
    edge_seed = edge_cotangent.reshape(peers, slots, width)
    receivers = edge_receiver.reshape(peers, 1, slots)
    live = live_counts.reshape(peers)
    mine = lax.axis_index("dev")
    paired = lax.axis_size("dev") == 8 and lax.axis_size("grp") == 4
    if paired:
        owners = jnp.arange(peers, dtype=jnp.int32) ^ mine
        order = chunk_order()
        index_rows = edge_sender.reshape(total_rows // width, width).astype(BF16)
        packed_nodes = jnp.concatenate(
            [nodes, jnp.pad(index_rows, ((0, 16 - index_rows.shape[0]), (0, 0)))]
        )
        gathered = gather_nodes(packed_nodes)
        tail = gathered[:, count : count + index_rows.shape[0]].reshape(peers, peers, slots)
        senders = lax.dynamic_index_in_dim(tail, mine, 1, keepdims=True).astype(jnp.int32)
    else:
        owners = jnp.arange(peers, dtype=jnp.int32)
        order = jnp.arange(CHUNKS, dtype=jnp.int32)
        gathered = lax.all_gather(nodes, "dev")
        senders = lax.all_to_all(
            edge_sender, "dev", split_axis=0, concat_axis=1, tiled=True
        ).reshape(peers, 1, slots)
    gathered_rows = gathered.shape[1]

    bias_row = edge_bias.reshape(1, width)
    gain_row = edge_gain.reshape(1, width)

    owned = pl.BlockSpec((1, slots, width), lambda i: (i, 0, 0))
    pre = pl.pallas_call(
        lift_kernel,
        grid=(peers,),
        in_specs=[
            owned,
            pl.BlockSpec((1, 1, slots), lambda i: (i, 0, 0)),
            whole(count, width),
            whole(3 * width, width),
            whole(1, width),
        ],
        out_specs=owned,
        out_shape=shape(peers, slots, width),
        compiler_params=params(24),
        cost_estimate=pl.CostEstimate(
            flops=5 * unit, bytes_accessed=6 * total_rows * width, transcendentals=0
        ),
        name="lift",
    )(edges, receivers, nodes, edge_lift, bias_row)

    def by_owner(*dims):
        return pl.BlockSpec(
            (1,) + dims, lambda i, owner, live, order: (owner[i],) + (0,) * len(dims)
        )

    def by_step(*dims):
        return pl.BlockSpec((1,) + dims, lambda i, *_: (i,) + (0,) * len(dims))

    hidden, normed, slope, inverse, base, summed_grad, node_packed, node_small = pl.pallas_call(
        forward_kernel,
        grid_spec=pltpu.PrefetchScalarGridSpec(
            num_scalar_prefetch=3,
            grid=(peers,),
            in_specs=[
                by_owner(slots, width),
                by_step(gathered_rows, width),
                by_step(1, slots),
                by_owner(1, slots),
                whole(count, width),
                whole(count, width),
                pl.BlockSpec((width, width), lambda *_: (1, 0)),
                whole(width, width),
                whole(1, width),
                whole(2 * width, width),
                whole(1, width),
                whole(width, width),
                whole(1, width),
            ],
            out_specs=[
                by_step(slots, width),
                by_step(slots, width),
                by_step(slots, width),
                by_step(slots, 1),
                whole(count, width),
                whole(count, width),
                whole(3 * width, width),
                whole(2, width),
            ],
            scratch_shapes=[pltpu.VMEM((count, width), F32), pltpu.VMEM((3 * width, width), F32)],
        ),
        out_shape=[
            shape(peers, slots, width, kind=BF16),
            shape(peers, slots, width, kind=BF16),
            shape(peers, slots, width, kind=BF16),
            shape(peers, slots, 1),
            shape(count, width),
            shape(count, width, kind=BF16),
            shape(3 * width, width, kind=BF16),
            shape(2, width),
        ],
        compiler_params=params(32),
        cost_estimate=pl.CostEstimate(
            flops=8 * unit, bytes_accessed=16 * total_rows * width, transcendentals=total_rows * width
        ),
        name="forward",
    )(
        owners,
        live,
        order,
        pre,
        gathered,
        senders,
        receivers,
        nodes,
        node_cotangent[0],
        edge_lift,
        edge_mix,
        gain_row,
        node_lift,
        node_bias.reshape(1, width),
        node_mix,
        node_gain.reshape(1, width),
    )

    grad_edges, partial, grad_nodes, edge_packed, edge_small = pl.pallas_call(
        backward_kernel,
        grid_spec=pltpu.PrefetchScalarGridSpec(
            num_scalar_prefetch=3,
            grid=(peers,),
            in_specs=[
                by_owner(slots, width),
                by_owner(slots, width),
                by_step(gathered_rows, width),
                by_step(1, slots),
                by_owner(1, slots),
                by_step(slots, width),
                by_step(slots, width),
                by_step(slots, width),
                by_step(slots, 1),
                whole(count, width),
                whole(count, width),
                whole(count, width),
                whole(3 * width, width),
                whole(width, width),
                whole(1, width),
            ],
            out_specs=[
                by_owner(slots, width),
                pl.BlockSpec((1, 1, count, width), lambda i, *_: (i % 2, i // 2, 0, 0)),
                whole(count, width),
                whole(4 * width, width),
                whole(2, width),
            ],
            scratch_shapes=[pltpu.VMEM((count, width), F32), pltpu.VMEM((4 * width, width), F32)],
        ),
        out_shape=[
            shape(peers, slots, width, kind=BF16),
            shape(2, peers // 2, count, width, kind=BF16),
            shape(count, width),
            shape(4 * width, width, kind=BF16),
            shape(2, width),
        ],
        compiler_params=params(40),
        cost_estimate=pl.CostEstimate(
            flops=14 * unit, bytes_accessed=20 * total_rows * width, transcendentals=0
        ),
        name="backward",
    )(
        owners,
        live,
        order,
        edges,
        edge_seed,
        gathered,
        senders,
        receivers,
        hidden,
        normed,
        slope,
        inverse,
        nodes,
        base,
        summed_grad,
        edge_lift,
        edge_mix,
        gain_row,
    )

    small = jnp.concatenate([edge_small, node_small])
    if paired:
        node_parts = reduce_plane(node_packed)
        edge_parts = reduce_plane(edge_packed)
        sizes = [part.shape[0] for part in node_parts[:1] + edge_parts[:1]]
        lined = reduce_line(node_parts + edge_parts)
        sides = spread_plane([jnp.concatenate([lined[0], lined[2]]), jnp.concatenate([lined[1], lined[3]])])
        node_side, edge_side = [], []
        for side in sides:
            pieces = split_rows(side, sizes * 4)
            node_side += pieces[0::2]
            edge_side += pieces[1::2]
        own = jnp.concatenate(node_side + edge_side)
        other = swap(own, "dev", 1)
        node_half = node_packed.shape[0] // 2
        node_sum = jnp.concatenate([own[:node_half], other[:node_half]])
        edge_sum = jnp.concatenate([own[node_half:], other[node_half:]])
        small = small_sum(small)
        from_senders = reduce_senders(partial)
    else:
        node_sum, edge_sum, small = lax.psum((node_packed.astype(F32), edge_packed.astype(F32), small), ("grp", "dev"))
        ordered = jnp.swapaxes(partial, 0, 1).reshape(peers, count, width)
        from_senders = lax.psum_scatter(ordered.astype(F32), "dev", scatter_dimension=0)
    grad_nodes = grad_nodes + contract_features(
        from_senders.astype(BF16), edge_lift[width : 2 * width]
    )
    groups = lax.axis_size("grp") * lax.axis_size("dev")
    edge_scale = float(total_rows * groups) ** (-0.5)
    node_scale = float(count * groups) ** (-0.5)
    edge_lift_grad, edge_mix_grad, node_lift_grad, node_mix_grad = pl.pallas_call(
        lambda *refs: unpack_kernel((edge_scale, node_scale), *refs),
        grid_spec=pltpu.PrefetchScalarGridSpec(
            num_scalar_prefetch=1,
            grid=(1,),
            in_specs=[whole(3 * width, width), whole(4 * width, width)],
            out_specs=[
                whole(3 * width, width),
                whole(width, width),
                whole(2 * width, width),
                whole(width, width),
            ],
            scratch_shapes=[
                pltpu.VMEM((4 * width, width), F32),
                pltpu.VMEM((3 * width, width), F32),
            ],
        ),
        out_shape=[
            shape(3 * width, width),
            shape(width, width),
            shape(2 * width, width),
            shape(width, width),
        ],
        compiler_params=params(48),
        name="unpack",
    )(order, node_sum, edge_sum)
    return (
        grad_nodes[None],
        grad_edges.reshape(1, 1, peers, slots, width),
        edge_lift_grad,
        small[0] * edge_scale,
        edge_mix_grad,
        small[1] * edge_scale,
        node_lift_grad,
        small[2] * node_scale,
        node_mix_grad,
        small[3] * node_scale,
    )


def solution(mesh):
    return jax.shard_map(
        per_device,
        mesh=mesh,
        in_specs=(
            P("grp", "dev", None),
            P("grp", "dev", None, None, None),
            P("grp", "dev", None),
            P("grp", "dev", None, None, None),
            P(None, "dev", None),
            P("dev", None, None),
            P("dev", None),
            P(),
            P(),
            P(),
            P(),
            P(),
            P(),
            P(),
            P(),
        ),
        out_specs=(
            P("grp", "dev", None),
            P("grp", "dev", None, None, None),
            P(),
            P(),
            P(),
            P(),
            P(),
            P(),
            P(),
            P(),
        ),
        check_vma=False,
    )
```

```python
import functools

import jax
import jax.numpy as jnp
from jax import lax
from jax.experimental import pallas as pl
from jax.experimental.pallas import tpu as pltpu
from jax.sharding import PartitionSpec as P

EPSILON = 1e-05
CHUNKS = 32
BF16 = jnp.bfloat16
F32 = jnp.float32


def matmul(left, right):
    return jnp.dot(left, right, preferred_element_type=F32)


def contract_rows(left, right):
    return lax.dot_general(left, right, (((0,), (0,)), ((), ())), preferred_element_type=F32)


def contract_features(left, right):
    return lax.dot_general(left, right, (((1,), (1,)), ((), ())), preferred_element_type=F32)


def one_hot(index_row, nodes):
    rows = lax.broadcasted_iota(jnp.int32, (nodes, index_row.shape[1]), 0)
    return jnp.where(rows == index_row, 1.0, 0.0).astype(BF16)


def silu_pair(values):
    gate = 0.5 * jnp.tanh(0.5 * values) + 0.5
    hidden = values * gate
    return hidden, gate + hidden * (1.0 - gate)


def norm_forward(values):
    centred = values - jnp.mean(values, axis=-1, keepdims=True)
    inverse = lax.rsqrt(jnp.mean(centred * centred, axis=-1, keepdims=True) + EPSILON)
    return centred * inverse, inverse


def norm_backward(grad_hat, normed, inverse):
    spread = jnp.mean(grad_hat * normed, axis=-1, keepdims=True)
    return inverse * (grad_hat - jnp.mean(grad_hat, axis=-1, keepdims=True) - normed * spread)


def pick_row(block, place):
    rows = lax.broadcasted_iota(jnp.int32, block.shape, 0)
    picked = jnp.sum(jnp.where(rows == place, block.astype(F32), 0.0), axis=0, keepdims=True)
    return picked.astype(jnp.int32)


def pack_kernel(nodes_ref, sender_ref, packed_ref):
    count, width = nodes_ref.shape
    peers, _, slots = sender_ref.shape
    packed_ref[:count] = nodes_ref[...]
    packed_ref[count:] = jnp.zeros((packed_ref.shape[0] - count, width), BF16)
    packed_ref[count : count + peers, :slots] = sender_ref[:, 0, :].astype(F32).astype(BF16)


def live_rows(count, shape):
    return lax.broadcasted_iota(jnp.int32, shape, 0) < count


def store_chunks(order_ref, source_ref, target_ref, mix_rows):
    mix_part = mix_rows // CHUNKS
    rows = source_ref.shape[0] // CHUNKS
    lift_part = rows - mix_part
    lift_rows = lift_part * CHUNKS

    def step(place, carry):
        chunk = order_ref[place]
        target = pl.multiple_of(place * rows, 16)
        lift_start = pl.multiple_of(chunk * lift_part, 16)
        mix_start = pl.multiple_of(lift_rows + chunk * mix_part, 16)
        target_ref[pl.ds(target, lift_part), :] = source_ref[
            pl.ds(lift_start, lift_part), :
        ].astype(BF16)
        target_ref[pl.ds(pl.multiple_of(target + lift_part, 16), mix_part), :] = source_ref[
            pl.ds(mix_start, mix_part), :
        ].astype(BF16)
        return carry

    lax.fori_loop(0, CHUNKS, step, 0)


def lift_kernel(edges_ref, receiver_ref, nodes_ref, lift_ref, bias_ref, pre_ref):
    width = nodes_ref.shape[1]
    table = one_hot(receiver_ref[pl.ds(pl.program_id(0), 1), :], nodes_ref.shape[0])
    receivers = contract_rows(table, nodes_ref[...]).astype(BF16)
    pre_ref[0] = (
        matmul(edges_ref[0], lift_ref[:width])
        + matmul(receivers, lift_ref[2 * width :])
        + bias_ref[...]
    )


def by_live(count, slots, body):
    part = slots // 4
    for quarter in range(1, 5):
        low = (quarter - 1) * part if quarter > 1 else -1

        @pl.when((count > low) & (count <= quarter * part))
        def _(rows=quarter * part):
            body(rows)


def load_pieces(step, sources, held_ref, sems):
    copies, start = [], 0
    for place, source in enumerate(sources):
        size = source.shape[0]
        copies.append(
            (start, pltpu.make_async_copy(source, held_ref.at[pl.ds(start, size)], sems.at[place]))
        )
        start += size

    @pl.when(step == 0)
    def _():
        for _, copy in copies:
            copy.start()

    for first, copy in copies:

        @pl.when(step == first)
        def _(copy=copy):
            copy.wait()


def forward_kernel(pieces, first, last, *refs):
    refs = list(refs)
    take = lambda size: [refs.pop(0) for _ in range(size)]
    owner_ref, live_ref, order_ref, mine_ref = take(4)
    sources = take(pieces)
    pre_ref, receiver_ref, nodes_ref, lift_ref, mix_ref, gain_ref = take(6)
    if not first:
        take(4)
        (carried_ref,) = take(1)
    if last:
        seed_ref, node_lift_hbm, node_bias_ref, node_mix_hbm, node_gain_ref = take(5)
    hidden_ref, normed_ref, slope_ref, inverse_ref = take(4)
    if last:
        base_ref, summed_grad_ref, packed_ref, small_ref = take(4)
    else:
        (summed_ref,) = take(1)
    held_ref, sems = take(2)
    if last:
        summed_ref, total_ref, node_lift_ref, node_mix_ref, weight_sems = take(5)
    step = pl.program_id(0)
    count, width = nodes_ref.shape
    load_pieces(step, sources, held_ref, sems)
    if last:
        loads = [
            pltpu.make_async_copy(node_lift_hbm, node_lift_ref, weight_sems.at[0]),
            pltpu.make_async_copy(node_mix_hbm, node_mix_ref, weight_sems.at[1]),
        ]

    @pl.when(step == 0)
    def _():
        if last:
            for load in loads:
                load.start()
        summed_ref[...] = jnp.zeros_like(summed_ref) if first else carried_ref[...]

    owner = owner_ref[step]
    live_count = live_ref[owner]

    def body(rows):
        index = pick_row(held_ref[step, count:, :rows], mine_ref[0])
        senders = contract_rows(one_hot(index, count), held_ref[step, :count]).astype(BF16)
        pre = pre_ref[0, :rows] + matmul(senders, lift_ref[...])
        hidden, slope = silu_pair(pre)
        hidden = hidden.astype(BF16)
        normed, inverse = norm_forward(matmul(hidden, mix_ref[...]))
        hidden_ref[0, :rows] = hidden
        slope_ref[0, :rows] = slope.astype(BF16)
        normed_ref[0, :rows] = normed.astype(BF16)
        inverse_ref[0, :rows] = inverse
        live = live_rows(live_count, normed.shape)
        message = jnp.where(live, normed * gain_ref[...], 0.0).astype(BF16)
        summed_ref[...] += matmul(one_hot(receiver_ref[pl.ds(owner, 1), :][:, :rows], count), message)

    by_live(live_count, pre_ref.shape[1], body)

    if not last:
        return

    @pl.when(step == pl.num_programs(0) - 1)
    def _():
        for load in loads:
            load.wait()
        nodes = nodes_ref[...]
        summed = summed_ref[...].astype(BF16)
        pre_node = (
            matmul(nodes, node_lift_ref[:width])
            + matmul(summed, node_lift_ref[width:])
            + node_bias_ref[...]
        )
        hidden_node, slope_node = silu_pair(pre_node)
        hidden_node = hidden_node.astype(BF16)
        normed_node, inverse_node = norm_forward(matmul(hidden_node, node_mix_ref[...]))
        seed = seed_ref[...].astype(F32)
        small_ref[1:2, :] = jnp.sum(seed * normed_node, axis=0, keepdims=True)
        grad_out = norm_backward(seed * node_gain_ref[...], normed_node, inverse_node).astype(BF16)
        total_ref[2 * width :, :] = contract_rows(hidden_node, grad_out)
        grad_pre = (contract_features(grad_out, node_mix_ref[...]) * slope_node).astype(BF16)
        small_ref[0:1, :] = jnp.sum(grad_pre.astype(F32), axis=0, keepdims=True)
        total_ref[:width, :] = contract_rows(nodes, grad_pre)
        total_ref[width : 2 * width, :] = contract_rows(summed, grad_pre)
        base_ref[...] = seed + contract_features(grad_pre, node_lift_ref[:width])
        summed_grad_ref[...] = contract_features(grad_pre, node_lift_ref[width:]).astype(BF16)
        store_chunks(order_ref, total_ref, packed_ref, width)


def backward_kernel(pieces, *refs):
    owner_ref, live_ref, order_ref, mine_ref = refs[:4]
    sources = refs[4 : 4 + pieces]
    (
        edges_ref,
        seed_ref,
        receiver_ref,
        hidden_ref,
        normed_ref,
        slope_ref,
        inverse_ref,
        nodes_ref,
        base_ref,
        summed_grad_ref,
        lift_ref,
        mix_ref,
        gain_ref,
        grad_edges_ref,
        partial_ref,
        grad_nodes_ref,
        packed_ref,
        small_ref,
        received_ref,
        total_ref,
        held_ref,
        sems,
    ) = refs[4 + pieces :]
    step = pl.program_id(0)
    count, width = nodes_ref.shape
    slots = edges_ref.shape[1]
    owner = owner_ref[step]
    live_count = live_ref[owner]
    load_pieces(step, sources, held_ref, sems)

    @pl.when(step == 0)
    def _():
        received_ref[...] = jnp.zeros_like(received_ref)
        total_ref[...] = jnp.zeros_like(total_ref)
        small_ref[...] = jnp.zeros_like(small_ref)

    def body(rows):
        seed = seed_ref[0, :rows].astype(F32)
        live = live_rows(live_count, seed.shape)
        receiver_table = one_hot(receiver_ref[pl.ds(owner, 1), :][:, :rows], count)
        grad_message = jnp.where(
            live, seed + contract_rows(receiver_table, summed_grad_ref[...]), 0.0
        )
        normed = normed_ref[0, :rows].astype(F32)
        small_ref[1:2, :] += jnp.sum(grad_message * normed, axis=0, keepdims=True)
        grad_out = norm_backward(
            grad_message * gain_ref[...], normed, inverse_ref[0, :rows]
        ).astype(BF16)
        total_ref[3 * width :, :] += contract_rows(hidden_ref[0, :rows], grad_out)
        grad_pre = (
            contract_features(grad_out, mix_ref[...]) * slope_ref[0, :rows].astype(F32)
        ).astype(BF16)
        small_ref[0:1, :] += jnp.sum(grad_pre.astype(F32), axis=0, keepdims=True)
        total_ref[:width, :] += contract_rows(edges_ref[0, :rows], grad_pre)
        index = pick_row(held_ref[step, count:, :rows], mine_ref[0])
        sent = matmul(one_hot(index, count), grad_pre).astype(BF16)
        partial_ref[0, 0] = sent
        total_ref[width : 2 * width, :] += contract_rows(held_ref[step, :count], sent)
        received_ref[...] += matmul(receiver_table, grad_pre)
        grad_edges_ref[0, :rows] = jnp.where(
            live, seed + contract_features(grad_pre, lift_ref[:width]), 0.0
        ).astype(BF16)
        if rows < slots:
            grad_edges_ref[0, rows:] = jnp.zeros((slots - rows, width), BF16)

    by_live(live_count, slots, body)

    @pl.when(step == pl.num_programs(0) - 1)
    def _():
        received = received_ref[...].astype(BF16)
        total_ref[2 * width : 3 * width, :] = contract_rows(nodes_ref[...], received)
        grad_nodes_ref[...] = base_ref[...] + contract_features(received, lift_ref[2 * width :])
        store_chunks(order_ref, total_ref, packed_ref, width)


def unpack_kernel(scale, pieces, place, *refs):
    order_ref = refs[0]
    sources = refs[1 : 1 + pieces]
    targets = refs[-9:-5]
    buffers = refs[-5:-1]
    sems = refs[-1]
    parts = [target.shape[0] // CHUNKS for target in targets]
    copies, slot = [], 0
    for source in sources:
        for start in range(0, source.shape[0], sum(parts)):
            for kind, rows in enumerate(parts):
                held = buffers[kind].at[pl.ds(slot * rows, rows)]
                held[...] = source[start : start + rows, :].astype(F32) * scale[kind // 2]
                target = pl.multiple_of(order_ref[place + slot] * rows, 16)
                copies.append(
                    pltpu.make_async_copy(
                        held, targets[kind].at[pl.ds(target, rows)], sems.at[kind, slot]
                    )
                )
                copies[-1].start()
                start += rows
            slot += 1
    for copy in copies:
        copy.wait()


def swap(values, axis, bit):
    size = lax.axis_size(axis)
    return lax.ppermute(values, axis, [(i, i ^ bit) for i in range(size)])


def add_rounded(left, right):
    return (left.astype(F32) + right.astype(F32)).astype(BF16)


def exchange(*moves):
    values = lax.optimization_barrier(tuple(move[0] for move in moves))
    moved = [swap(value, axis, bit) for value, (_, axis, bit) in zip(values, moves)]
    return lax.optimization_barrier(tuple(moved))


def halves(part):
    rows = part.shape[0] // 2
    return part[:rows], part[rows:]


def join(*parts):
    return jnp.concatenate(parts)


def reduce_all(edge_packed, node_packed, partial, small):
    side_a, side_b = halves(node_packed)
    keep_a, send_a = halves(side_a)
    keep_b, send_b = halves(side_b)
    got_a, got_b = swap(send_a, "grp", 1), swap(send_b, "grp", 2)
    node_a, node_b = add_rounded(keep_a, got_a), add_rounded(keep_b, got_b)

    keep, send = halves(edge_packed)
    got, got_small = exchange((send, "dev", 1), (small, "dev", 1))
    edge_a, edge_b = halves(add_rounded(keep, got))
    small = small + got_small

    keep_a, send_a = halves(edge_a)
    keep_b, send_b = halves(edge_b)
    node_keep_a, node_send_a = halves(node_a)
    node_keep_b, node_send_b = halves(node_b)
    got_a, got_b, got_node, got_small, got_partial = exchange(
        (send_a, "grp", 1),
        (send_b, "grp", 2),
        (join(node_send_a, node_send_b), "dev", 1),
        (small, "grp", 1),
        (partial[1], "dev", 1),
    )
    owned = add_rounded(partial[0], got_partial)
    edge_a, edge_b = add_rounded(keep_a, got_a), add_rounded(keep_b, got_b)
    got_node_a, got_node_b = halves(got_node)
    node_a, node_b = add_rounded(node_keep_a, got_node_a), add_rounded(node_keep_b, got_node_b)
    small = small + got_small

    pairs = [halves(part) for part in (edge_a, node_a, edge_b, node_b)]
    got_a, got_b, got_small = exchange(
        (join(pairs[0][1], pairs[1][1]), "grp", 2),
        (join(pairs[2][1], pairs[3][1]), "grp", 1),
        (small, "grp", 2),
    )
    small = small + got_small
    edge_rows = pairs[0][0].shape[0]
    parts = [
        add_rounded(pairs[0][0], got_a[:edge_rows]),
        add_rounded(pairs[1][0], got_a[edge_rows:]),
        add_rounded(pairs[2][0], got_b[:edge_rows]),
        add_rounded(pairs[3][0], got_b[edge_rows:]),
    ]
    pairs = [halves(part) for part in parts]
    got, got_small = exchange((join(*[pair[1] for pair in pairs]), "dev", 2), (small, "dev", 2))
    kept = add_rounded(join(*[pair[0] for pair in pairs]), got)
    small = small + got_small
    got, got_small, got_owned = exchange(
        (kept, "dev", 4), (small, "dev", 4), (owned[1::2], "dev", 2)
    )
    owned = add_rounded(owned[::2], got_owned)
    kept = add_rounded(kept, got)
    small = small + got_small
    early_rows, late_rows = halves(owned[1])
    other, got_early = exchange((kept, "dev", 2), (early_rows, "dev", 4))

    (own_a, own_b), (other_a, other_b) = halves(kept), halves(other)
    side_a, side_b = join(own_a, other_a), join(own_b, other_b)
    got_a, got_b, got_late = exchange(
        (side_a, "grp", 2), (side_b, "grp", 1), (late_rows, "dev", 4)
    )
    from_senders = owned[0].astype(F32) + join(got_early, got_late).astype(F32)
    side_a, side_b = join(side_a, got_a), join(side_b, got_b)
    got_a, got_b, swapped_a, swapped_b = exchange(
        (side_a, "grp", 1),
        (side_b, "grp", 2),
        (side_a, "dev", 1),
        (side_b, "dev", 1),
    )
    last_a, last_b = exchange((got_a, "dev", 1), (got_b, "dev", 1))
    ordered = [[side_a, got_a, side_b, got_b], [swapped_a, last_a, swapped_b, last_b]]
    return ordered, small, from_senders


def device_bits():
    group = lax.axis_index("grp")
    device = lax.axis_index("dev")
    return group & 1, group >> 1, device & 1, (device >> 1) & 1


def relative_places(place):
    x, y, core, z = device_bits()
    first = core * 16 + x * 4 + y * 2 + z
    second = core * 16 + y * 4 + x * 2 + z
    return place ^ jnp.where((place & 8) == 0, first, second)


def edge_order():
    return relative_places(jnp.arange(CHUNKS, dtype=jnp.int32))


def node_order():
    place = jnp.arange(CHUNKS, dtype=jnp.int32)
    return relative_places(((place & 4) << 2) | ((place & 24) >> 1) | (place & 3))


def shape(*dims, kind=F32):
    return jax.ShapeDtypeStruct(dims, kind)


def params(mebibytes):
    return pltpu.CompilerParams(vmem_limit_bytes=mebibytes << 20)


def whole(*dims):
    return pl.BlockSpec(dims, lambda *_: (0,) * len(dims), pipeline_mode=pl.Buffered(1))


def result(*dims):
    return pl.BlockSpec(dims, lambda *_: (0,) * len(dims))


def per_device(
    node_latent,
    edge_latent,
    node_cotangent,
    edge_cotangent,
    edge_sender,
    edge_receiver,
    live_counts,
    edge_lift,
    edge_bias,
    edge_mix,
    edge_gain,
    node_lift,
    node_bias,
    node_mix,
    node_gain,
):
    width = node_latent.shape[2]
    nodes = node_latent[0]
    count = nodes.shape[0]
    peers = edge_receiver.shape[1]
    slots = edge_receiver.shape[2]
    total_rows = peers * slots
    unit = total_rows * width * width
    edges = edge_latent.reshape(peers, slots, width)
    edge_seed = edge_cotangent.reshape(peers, slots, width)
    receivers = edge_receiver.reshape(peers, slots)
    live = live_counts.reshape(peers)
    mine = lax.axis_index("dev")
    paired = lax.axis_size("dev") == 8 and lax.axis_size("grp") == 4
    packed_rows = count + -(-peers // 16) * 16
    packed_nodes = pl.pallas_call(
        pack_kernel,
        out_shape=shape(packed_rows, width, kind=BF16),
        compiler_params=params(4),
        name="pack",
    )(nodes, edge_sender)
    if paired:
        owners = jnp.arange(peers, dtype=jnp.int32) ^ mine
        edge_places = edge_order()
        node_places = node_order()
        near = swap(packed_nodes, "dev", 2)
        far = [swap(packed_nodes, "dev", 4), swap(packed_nodes, "dev", 6)]
        pieces = [packed_nodes, swap(packed_nodes, "dev", 1), near, swap(near, "dev", 1)]
        pieces = [piece[None] for piece in pieces]
        ranges = [(0, 4), (4, 8)]
    else:
        owners = jnp.arange(peers, dtype=jnp.int32)
        edge_places = node_places = jnp.arange(CHUNKS, dtype=jnp.int32)
        pieces = [lax.all_gather(packed_nodes, "dev")]
        ranges = [(0, peers)]
    gathered_rows = pieces[0].shape[1]

    anywhere = pl.BlockSpec(memory_space=pl.ANY)
    bias_row = edge_bias.reshape(1, width)
    gain_row = edge_gain.reshape(1, width)

    owned = pl.BlockSpec((1, slots, width), lambda i: (i, 0, 0))
    pre = pl.pallas_call(
        lift_kernel,
        grid=(peers,),
        in_specs=[
            owned,
            whole(peers, slots),
            whole(count, width),
            whole(3 * width, width),
            whole(1, width),
        ],
        out_specs=owned,
        out_shape=shape(peers, slots, width),
        compiler_params=params(12),
        cost_estimate=pl.CostEstimate(
            flops=5 * unit, bytes_accessed=6 * total_rows * width, transcendentals=0
        ),
        name="lift",
    )(edges, receivers, nodes, edge_lift, bias_row)

    def by_owner(*dims):
        return pl.BlockSpec(
            (1,) + dims, lambda i, owner, *_: (owner[i],) + (0,) * len(dims)
        )

    def by_step(*dims):
        return pl.BlockSpec((1,) + dims, lambda i, *_: (i,) + (0,) * len(dims))

    saved = []
    summed = None
    for begin, end in ranges:
        first, last = begin == 0, end == peers
        if not first:
            *far, summed = lax.optimization_barrier((*far, summed))
            for piece in far:
                pieces += [piece[None], swap(piece, "dev", 1)[None]]
        chosen = pieces[begin:] if paired else pieces

        def saved_step(*dims, begin=begin):
            return pl.BlockSpec((1,) + dims, lambda i, *_: (i + begin,) + (0,) * len(dims))

        operands = chosen + [
            pre,
            receivers,
            nodes,
            edge_lift,
            edge_mix,
            gain_row,
        ]
        in_specs = [anywhere] * len(chosen) + [
            by_owner(slots, width),
            whole(peers, slots),
            whole(count, width),
            pl.BlockSpec((width, width), lambda *_: (1, 0), pipeline_mode=pl.Buffered(1)),
            whole(width, width),
            whole(1, width),
        ]
        aliases = {}
        if not first:
            aliases = {4 + len(operands) + j: j for j in range(4)}
            operands += saved + [summed]
            in_specs += [anywhere] * 4 + [whole(count, width)]
        out_specs = [saved_step(slots, width)] * 3 + [saved_step(slots, 1)]
        out_shape = [shape(peers, slots, width, kind=BF16)] * 3 + [shape(peers, slots, 1)]
        scratch = [
            pltpu.VMEM((end - begin, gathered_rows, width), BF16),
            pltpu.SemaphoreType.DMA((len(chosen),)),
        ]
        if last:
            operands += [
                node_cotangent[0],
                node_lift,
                node_bias.reshape(1, width),
                node_mix,
                node_gain.reshape(1, width),
            ]
            in_specs += [whole(count, width), anywhere, whole(1, width), anywhere, whole(1, width)]
            out_specs += [
                result(count, width),
                result(count, width),
                result(3 * width, width),
                result(2, width),
            ]
            out_shape += [
                shape(count, width),
                shape(count, width, kind=BF16),
                shape(3 * width, width, kind=BF16),
                shape(2, width),
            ]
            scratch += [
                pltpu.VMEM((count, width), F32),
                pltpu.VMEM((3 * width, width), F32),
                pltpu.VMEM((2 * width, width), BF16),
                pltpu.VMEM((width, width), BF16),
                pltpu.SemaphoreType.DMA((2,)),
            ]
        else:
            out_specs.append(result(count, width))
            out_shape.append(shape(count, width))
        results = pl.pallas_call(
            functools.partial(forward_kernel, len(chosen), first, last),
            grid_spec=pltpu.PrefetchScalarGridSpec(
                num_scalar_prefetch=4,
                grid=(end - begin,),
                in_specs=in_specs,
                out_specs=out_specs,
                scratch_shapes=scratch,
            ),
            out_shape=out_shape,
            input_output_aliases=aliases,
            compiler_params=params(24),
            cost_estimate=pl.CostEstimate(
                flops=4 * unit,
                bytes_accessed=8 * total_rows * width,
                transcendentals=total_rows * width,
            ),
            name="forward_" + ("all" if last else "near"),
        )(owners[begin:end], live, node_places, mine.reshape(1), *operands)
        saved = list(results[:4])
        if last:
            base, summed_grad, node_packed, node_small = results[4:]
        else:
            summed = results[4]
    hidden, normed, slope, inverse = saved

    grad_edges, partial, grad_nodes, edge_packed, edge_small = pl.pallas_call(
        functools.partial(backward_kernel, len(pieces)),
        grid_spec=pltpu.PrefetchScalarGridSpec(
            num_scalar_prefetch=4,
            grid=(peers,),
            in_specs=[anywhere] * len(pieces)
            + [
                by_owner(slots, width),
                by_owner(slots, width),
                whole(peers, slots),
                by_step(slots, width),
                by_step(slots, width),
                by_step(slots, width),
                by_step(slots, 1),
                whole(count, width),
                whole(count, width),
                whole(count, width),
                whole(3 * width, width),
                whole(width, width),
                whole(1, width),
            ],
            out_specs=[
                by_owner(slots, width),
                pl.BlockSpec((1, 1, count, width), lambda i, *_: (i % 2, i // 2, 0, 0)),
                result(count, width),
                result(4 * width, width),
                result(2, width),
            ],
            scratch_shapes=[
                pltpu.VMEM((count, width), F32),
                pltpu.VMEM((4 * width, width), F32),
                pltpu.VMEM((peers, gathered_rows, width), BF16),
                pltpu.SemaphoreType.DMA((len(pieces),)),
            ],
        ),
        out_shape=[
            shape(peers, slots, width, kind=BF16),
            shape(2, peers // 2, count, width, kind=BF16),
            shape(count, width),
            shape(4 * width, width, kind=BF16),
            shape(2, width),
        ],
        compiler_params=params(28),
        cost_estimate=pl.CostEstimate(
            flops=14 * unit, bytes_accessed=20 * total_rows * width, transcendentals=0
        ),
        name="backward",
    )(
        owners,
        live,
        edge_places,
        mine.reshape(1),
        *pieces,
        edges,
        edge_seed,
        receivers,
        hidden,
        normed,
        slope,
        inverse,
        nodes,
        base,
        summed_grad,
        edge_lift,
        edge_mix,
        gain_row,
    )

    small = jnp.concatenate([edge_small, node_small])
    if paired:
        sources, small, from_senders = reduce_all(edge_packed, node_packed, partial, small)
    else:
        node_sum, edge_sum, small = lax.psum(
            (node_packed.astype(F32), edge_packed.astype(F32), small), ("grp", "dev")
        )
        interleaved = jnp.concatenate(
            [
                edge_sum.reshape(CHUNKS, 4 * width // CHUNKS, width),
                node_sum.reshape(CHUNKS, 3 * width // CHUNKS, width),
            ],
            axis=1,
        )
        sources = [[interleaved.reshape(7 * width, width).astype(BF16)]]
        ordered = jnp.swapaxes(partial, 0, 1).reshape(peers, count, width)
        from_senders = lax.psum_scatter(ordered.astype(F32), "dev", scatter_dimension=0)
    grad_nodes = grad_nodes + contract_features(
        from_senders.astype(BF16), edge_lift[width : 2 * width]
    )
    groups = lax.axis_size("grp") * lax.axis_size("dev")
    edge_scale = float(total_rows * groups) ** (-0.5)
    node_scale = float(count * groups) ** (-0.5)
    totals = [3 * width, width, 2 * width, width]
    unpacked, place = [], 0
    for part in sources:
        places = sum(source.shape[0] for source in part) * CHUNKS // (7 * width)
        unpacked = pl.pallas_call(
            functools.partial(unpack_kernel, (edge_scale, node_scale), len(part), place),
            grid_spec=pltpu.PrefetchScalarGridSpec(
                num_scalar_prefetch=1,
                grid=(1,),
                in_specs=[whole(*source.shape) for source in part] + [anywhere] * len(unpacked),
                out_specs=[anywhere] * 4,
                scratch_shapes=[
                    pltpu.VMEM((places * total // CHUNKS, width), F32) for total in totals
                ]
                + [pltpu.SemaphoreType.DMA((4, places))],
            ),
            out_shape=[shape(total, width) for total in totals],
            input_output_aliases={1 + len(part) + j: j for j in range(len(unpacked))},
            compiler_params=params(20),
            cost_estimate=pl.CostEstimate(
                flops=0, bytes_accessed=42 * places * width * width // CHUNKS, transcendentals=0
            ),
            name="unpack_%d" % place,
        )(edge_places, *part, *unpacked)
        place += places
    edge_lift_grad, edge_mix_grad, node_lift_grad, node_mix_grad = unpacked
    return (
        grad_nodes[None],
        grad_edges.reshape(1, 1, peers, slots, width),
        edge_lift_grad,
        small[0] * edge_scale,
        edge_mix_grad,
        small[1] * edge_scale,
        node_lift_grad,
        small[2] * node_scale,
        node_mix_grad,
        small[3] * node_scale,
    )


def solution(mesh):
    return jax.shard_map(
        per_device,
        mesh=mesh,
        in_specs=(
            P("grp", "dev", None),
            P("grp", "dev", None, None, None),
            P("grp", "dev", None),
            P("grp", "dev", None, None, None),
            P(None, "dev", None),
            P("dev", None, None),
            P("dev", None),
            P(),
            P(),
            P(),
            P(),
            P(),
            P(),
            P(),
            P(),
        ),
        out_specs=(
            P("grp", "dev", None),
            P("grp", "dev", None, None, None),
            P(),
            P(),
            P(),
            P(),
            P(),
            P(),
            P(),
            P(),
        ),
        check_vma=False,
    )
```

```python
import functools

import jax
import jax.numpy as jnp
from jax import lax
from jax.experimental import pallas as pl
from jax.experimental.pallas import tpu as pltpu
from jax.sharding import PartitionSpec as P

EPSILON = 1e-05
CHUNKS = 32
BF16 = jnp.bfloat16
F32 = jnp.float32


def matmul(left, right):
    return jnp.dot(left, right, preferred_element_type=F32)


def contract_rows(left, right):
    return lax.dot_general(left, right, (((0,), (0,)), ((), ())), preferred_element_type=F32)


def contract_features(left, right):
    return lax.dot_general(left, right, (((1,), (1,)), ((), ())), preferred_element_type=F32)


def one_hot(index_row, nodes):
    rows = lax.broadcasted_iota(jnp.int32, (nodes, index_row.shape[1]), 0)
    return jnp.where(rows == index_row, 1.0, 0.0).astype(BF16)


def silu_pair(values):
    gate = 0.5 * jnp.tanh(0.5 * values) + 0.5
    hidden = values * gate
    return hidden, gate + hidden * (1.0 - gate)


def norm_forward(values):
    centred = values - jnp.mean(values, axis=-1, keepdims=True)
    inverse = lax.rsqrt(jnp.mean(centred * centred, axis=-1, keepdims=True) + EPSILON)
    return centred * inverse, inverse


def norm_backward(grad_hat, normed, inverse):
    spread = jnp.mean(grad_hat * normed, axis=-1, keepdims=True)
    return inverse * (grad_hat - jnp.mean(grad_hat, axis=-1, keepdims=True) - normed * spread)


def pick_row(block, place):
    rows = lax.broadcasted_iota(jnp.int32, block.shape, 0)
    picked = jnp.sum(jnp.where(rows == place, block.astype(F32), 0.0), axis=0, keepdims=True)
    return picked.astype(jnp.int32)


def pack_kernel(nodes_ref, sender_ref, packed_ref):
    count, width = nodes_ref.shape
    peers, _, slots = sender_ref.shape
    packed_ref[:count] = nodes_ref[...]
    packed_ref[count:] = jnp.zeros((packed_ref.shape[0] - count, width), BF16)
    packed_ref[count : count + peers, :slots] = sender_ref[:, 0, :].astype(F32).astype(BF16)


def live_rows(count, shape):
    return lax.broadcasted_iota(jnp.int32, shape, 0) < count


def store_chunks(order_ref, source_ref, target_ref, mix_rows):
    mix_part = mix_rows // CHUNKS
    rows = source_ref.shape[0] // CHUNKS
    lift_part = rows - mix_part
    lift_rows = lift_part * CHUNKS

    def step(place, carry):
        chunk = order_ref[place]
        target = pl.multiple_of(place * rows, 16)
        lift_start = pl.multiple_of(chunk * lift_part, 16)
        mix_start = pl.multiple_of(lift_rows + chunk * mix_part, 16)
        target_ref[pl.ds(target, lift_part), :] = source_ref[
            pl.ds(lift_start, lift_part), :
        ].astype(BF16)
        target_ref[pl.ds(pl.multiple_of(target + lift_part, 16), mix_part), :] = source_ref[
            pl.ds(mix_start, mix_part), :
        ].astype(BF16)
        return carry

    lax.fori_loop(0, CHUNKS, step, 0)


def lift_kernel(edges_ref, receiver_ref, nodes_ref, lift_ref, bias_ref, pre_ref):
    width = nodes_ref.shape[1]
    table = one_hot(receiver_ref[pl.ds(pl.program_id(0), 1), :], nodes_ref.shape[0])
    receivers = contract_rows(table, nodes_ref[...]).astype(BF16)
    pre_ref[0] = (
        matmul(edges_ref[0], lift_ref[:width])
        + matmul(receivers, lift_ref[2 * width :])
        + bias_ref[...]
    )


def by_live(count, slots, body):
    part = slots // 4
    for quarter in range(1, 5):
        low = (quarter - 1) * part if quarter > 1 else -1

        @pl.when((count > low) & (count <= quarter * part))
        def _(rows=quarter * part):
            body(rows)


def load_pieces(step, sources, held_ref, sems):
    copies, start = [], 0
    for place, source in enumerate(sources):
        size = source.shape[0]
        copies.append(
            (start, pltpu.make_async_copy(source, held_ref.at[pl.ds(start, size)], sems.at[place]))
        )
        start += size

    @pl.when(step == 0)
    def _():
        for _, copy in copies:
            copy.start()

    for first, copy in copies:

        @pl.when(step == first)
        def _(copy=copy):
            copy.wait()


def forward_kernel(pieces, first, last, *refs):
    refs = list(refs)
    take = lambda size: [refs.pop(0) for _ in range(size)]
    owner_ref, live_ref, order_ref, mine_ref = take(4)
    sources = take(pieces)
    pre_ref, receiver_ref, nodes_ref, lift_ref, mix_ref, gain_ref = take(6)
    if not first:
        take(4)
        (carried_ref,) = take(1)
    if last:
        seed_ref, node_lift_hbm, node_bias_ref, node_mix_hbm, node_gain_ref = take(5)
    hidden_ref, normed_ref, slope_ref, inverse_ref = take(4)
    if last:
        base_ref, summed_grad_ref, packed_ref, small_ref = take(4)
    else:
        (summed_ref,) = take(1)
    held_ref, sems = take(2)
    if last:
        summed_ref, total_ref, node_lift_ref, node_mix_ref, weight_sems = take(5)
    step = pl.program_id(0)
    count, width = nodes_ref.shape
    load_pieces(step, sources, held_ref, sems)
    if last:
        loads = [
            pltpu.make_async_copy(node_lift_hbm, node_lift_ref, weight_sems.at[0]),
            pltpu.make_async_copy(node_mix_hbm, node_mix_ref, weight_sems.at[1]),
        ]

    @pl.when(step == 0)
    def _():
        if last:
            for load in loads:
                load.start()
        summed_ref[...] = jnp.zeros_like(summed_ref) if first else carried_ref[...]

    owner = owner_ref[step]
    live_count = live_ref[owner]

    def body(rows):
        index = pick_row(held_ref[step, count:, :rows], mine_ref[0])
        senders = contract_rows(one_hot(index, count), held_ref[step, :count]).astype(BF16)
        pre = pre_ref[0, :rows] + matmul(senders, lift_ref[...])
        hidden, slope = silu_pair(pre)
        hidden = hidden.astype(BF16)
        normed, inverse = norm_forward(matmul(hidden, mix_ref[...]))
        hidden_ref[0, :rows] = hidden
        slope_ref[0, :rows] = slope.astype(BF16)
        normed_ref[0, :rows] = normed.astype(BF16)
        inverse_ref[0, :rows] = inverse
        live = live_rows(live_count, normed.shape)
        message = jnp.where(live, normed * gain_ref[...], 0.0).astype(BF16)
        summed_ref[...] += matmul(one_hot(receiver_ref[pl.ds(owner, 1), :][:, :rows], count), message)

    by_live(live_count, pre_ref.shape[1], body)

    if not last:
        return

    @pl.when(step == pl.num_programs(0) - 1)
    def _():
        for load in loads:
            load.wait()
        nodes = nodes_ref[...]
        summed = summed_ref[...].astype(BF16)
        pre_node = (
            matmul(nodes, node_lift_ref[:width])
            + matmul(summed, node_lift_ref[width:])
            + node_bias_ref[...]
        )
        hidden_node, slope_node = silu_pair(pre_node)
        hidden_node = hidden_node.astype(BF16)
        normed_node, inverse_node = norm_forward(matmul(hidden_node, node_mix_ref[...]))
        seed = seed_ref[...].astype(F32)
        small_ref[1:2, :] = jnp.sum(seed * normed_node, axis=0, keepdims=True)
        grad_out = norm_backward(seed * node_gain_ref[...], normed_node, inverse_node).astype(BF16)
        total_ref[2 * width :, :] = contract_rows(hidden_node, grad_out)
        grad_pre = (contract_features(grad_out, node_mix_ref[...]) * slope_node).astype(BF16)
        small_ref[0:1, :] = jnp.sum(grad_pre.astype(F32), axis=0, keepdims=True)
        total_ref[:width, :] = contract_rows(nodes, grad_pre)
        total_ref[width : 2 * width, :] = contract_rows(summed, grad_pre)
        base_ref[...] = seed + contract_features(grad_pre, node_lift_ref[:width])
        summed_grad_ref[...] = contract_features(grad_pre, node_lift_ref[width:]).astype(BF16)
        store_chunks(order_ref, total_ref, packed_ref, width)


def backward_kernel(pieces, *refs):
    owner_ref, live_ref, order_ref, mine_ref = refs[:4]
    sources = refs[4 : 4 + pieces]
    (
        edges_ref,
        seed_ref,
        receiver_ref,
        hidden_ref,
        normed_ref,
        slope_ref,
        inverse_ref,
        nodes_ref,
        base_ref,
        summed_grad_ref,
        lift_ref,
        mix_ref,
        gain_ref,
        grad_edges_ref,
        partial_ref,
        grad_nodes_ref,
        packed_ref,
        small_ref,
        received_ref,
        total_ref,
        held_ref,
        sems,
    ) = refs[4 + pieces :]
    step = pl.program_id(0)
    count, width = nodes_ref.shape
    slots = edges_ref.shape[1]
    owner = owner_ref[step]
    live_count = live_ref[owner]
    load_pieces(step, sources, held_ref, sems)

    @pl.when(step == 0)
    def _():
        received_ref[...] = jnp.zeros_like(received_ref)
        total_ref[...] = jnp.zeros_like(total_ref)
        small_ref[...] = jnp.zeros_like(small_ref)

    def body(rows):
        seed = seed_ref[0, :rows].astype(F32)
        live = live_rows(live_count, seed.shape)
        receiver_table = one_hot(receiver_ref[pl.ds(owner, 1), :][:, :rows], count)
        grad_message = jnp.where(
            live, seed + contract_rows(receiver_table, summed_grad_ref[...]), 0.0
        )
        normed = normed_ref[0, :rows].astype(F32)
        small_ref[1:2, :] += jnp.sum(grad_message * normed, axis=0, keepdims=True)
        grad_out = norm_backward(
            grad_message * gain_ref[...], normed, inverse_ref[0, :rows]
        ).astype(BF16)
        total_ref[3 * width :, :] += contract_rows(hidden_ref[0, :rows], grad_out)
        grad_pre = (
            contract_features(grad_out, mix_ref[...]) * slope_ref[0, :rows].astype(F32)
        ).astype(BF16)
        small_ref[0:1, :] += jnp.sum(grad_pre.astype(F32), axis=0, keepdims=True)
        total_ref[:width, :] += contract_rows(edges_ref[0, :rows], grad_pre)
        index = pick_row(held_ref[step, count:, :rows], mine_ref[0])
        sent = matmul(one_hot(index, count), grad_pre).astype(BF16)
        partial_ref[0, 0] = sent
        total_ref[width : 2 * width, :] += contract_rows(held_ref[step, :count], sent)
        received_ref[...] += matmul(receiver_table, grad_pre)
        grad_edges_ref[0, :rows] = jnp.where(
            live, seed + contract_features(grad_pre, lift_ref[:width]), 0.0
        ).astype(BF16)
        if rows < slots:
            grad_edges_ref[0, rows:] = jnp.zeros((slots - rows, width), BF16)

    by_live(live_count, slots, body)

    @pl.when(step == pl.num_programs(0) - 1)
    def _():
        received = received_ref[...].astype(BF16)
        total_ref[2 * width : 3 * width, :] = contract_rows(nodes_ref[...], received)
        grad_nodes_ref[...] = base_ref[...] + contract_features(received, lift_ref[2 * width :])
        store_chunks(order_ref, total_ref, packed_ref, width)


def unpack_kernel(scale, places, *refs):
    order_ref = refs[0]
    sources = refs[1 : 1 + len(places)]
    targets = refs[-9:-5]
    buffers = refs[-5:-1]
    sems = refs[-1]
    parts = [target.shape[0] // CHUNKS for target in targets]
    copies, slot = [], 0
    for source, place in zip(sources, places):
        for start in range(0, source.shape[0], sum(parts)):
            for kind, rows in enumerate(parts):
                held = buffers[kind].at[pl.ds(slot * rows, rows)]
                held[...] = source[start : start + rows, :].astype(F32) * scale[kind // 2]
                target = pl.multiple_of(order_ref[place] * rows, 16)
                copies.append(
                    pltpu.make_async_copy(
                        held, targets[kind].at[pl.ds(target, rows)], sems.at[kind, slot]
                    )
                )
                copies[-1].start()
                start += rows
            slot += 1
            place += 1
    for copy in copies:
        copy.wait()


def swap(values, axis, bit):
    size = lax.axis_size(axis)
    return lax.ppermute(values, axis, [(i, i ^ bit) for i in range(size)])


def add_rounded(left, right):
    return (left.astype(F32) + right.astype(F32)).astype(BF16)


def exchange(*moves):
    values = lax.optimization_barrier(tuple(move[0] for move in moves))
    moved = [swap(value, axis, bit) for value, (_, axis, bit) in zip(values, moves)]
    return lax.optimization_barrier(tuple(moved))


def halves(part):
    rows = part.shape[0] // 2
    return part[:rows], part[rows:]


def halves_inner(blocks):
    rows = blocks.shape[1] // 2
    return blocks[:, :rows], blocks[:, rows:]


def join(*parts):
    return jnp.concatenate(parts)


def node_start(node_packed):
    sides = [halves(side) for side in halves(node_packed)]
    got = [swap(sides[0][1], "grp", 1), swap(sides[1][1], "grp", 2)]
    return [side[0] for side in sides], got


def reduce_all(edge_packed, node_kept, node_got, partial, small):
    node_a, node_b = [add_rounded(kept, got) for kept, got in zip(node_kept, node_got)]

    keep, send = halves(edge_packed)
    got, got_small, got_partial = exchange(
        (send, "dev", 1), (small, "dev", 1), (partial[1], "dev", 1)
    )
    edge_a, edge_b = halves(add_rounded(keep, got))
    small = small + got_small
    owned = add_rounded(partial[0], got_partial)
    owned_early, owned_late = halves_inner(owned)

    keep_a, send_a = halves(edge_a)
    keep_b, send_b = halves(edge_b)
    node_keep_a, node_send_a = halves(node_a)
    node_keep_b, node_send_b = halves(node_b)
    got_a, got_b, got_node, got_small, got_owned = exchange(
        (send_a, "grp", 1),
        (send_b, "grp", 2),
        (join(node_send_a, node_send_b), "dev", 1),
        (small, "grp", 1),
        (owned_early[1::2], "dev", 2),
    )
    edge_a, edge_b = add_rounded(keep_a, got_a), add_rounded(keep_b, got_b)
    got_node_a, got_node_b = halves(got_node)
    node_a, node_b = add_rounded(node_keep_a, got_node_a), add_rounded(node_keep_b, got_node_b)
    small = small + got_small
    owned_early = add_rounded(owned_early[::2], got_owned)

    pairs = [halves(part) for part in (edge_a, node_a, edge_b, node_b)]
    got_a, got_b, got_small, got_owned, got_early = exchange(
        (join(pairs[0][1], pairs[1][1]), "grp", 2),
        (join(pairs[2][1], pairs[3][1]), "grp", 1),
        (small, "grp", 2),
        (owned_late[1::2], "dev", 2),
        (owned_early[1], "dev", 4),
    )
    small = small + got_small
    owned_late = add_rounded(owned_late[::2], got_owned)
    edge_rows = pairs[0][0].shape[0]
    parts = [
        halves(add_rounded(pairs[0][0], got_a[:edge_rows])),
        halves(add_rounded(pairs[1][0], got_a[edge_rows:])),
        halves(add_rounded(pairs[2][0], got_b[:edge_rows])),
        halves(add_rounded(pairs[3][0], got_b[edge_rows:])),
    ]
    got_1, got_2, got_3, got_small = exchange(
        (join(parts[0][1], parts[1][1]), "dev", 2),
        (join(parts[2][0], parts[3][0]), "dev", 4),
        (join(parts[2][1], parts[3][1]), "dev", 6),
        (small, "dev", 2),
    )
    small = small + got_small
    kept = sum(
        (got.astype(F32) for got in (got_1, got_2, got_3)),
        join(parts[0][0], parts[1][0]).astype(F32),
    ).astype(BF16)
    got_1, got_2, got_small = exchange((kept, "dev", 2), (kept, "dev", 4), (small, "dev", 4))
    (got_3,) = exchange((got_2, "dev", 2))
    small = small + got_small

    side_a, side_b = join(kept, got_1), join(got_2, got_3)
    got_a, got_b, got_late = exchange(
        (side_a, "grp", 2), (side_b, "grp", 1), (owned_late[1], "dev", 4)
    )
    from_senders = join(owned_early[0], owned_late[0]).astype(F32) + join(
        got_early, got_late
    ).astype(F32)
    side_a, side_b = join(side_a, got_a), join(side_b, got_b)
    got_a, got_b, swapped_a, swapped_b = exchange(
        (side_a, "grp", 1),
        (side_b, "grp", 2),
        (side_a, "dev", 1),
        (side_b, "dev", 1),
    )
    last_a, last_b = exchange((got_a, "dev", 1), (got_b, "dev", 1))
    sources = [
        [(side_a, 0), (side_b, 8)],
        [(got_a, 4), (got_b, 12), (swapped_a, 16), (swapped_b, 24)],
        [(last_a, 20), (last_b, 28)],
    ]
    return sources, small, from_senders


def device_bits():
    group = lax.axis_index("grp")
    device = lax.axis_index("dev")
    return group & 1, group >> 1, device & 1, (device >> 1) & 1, (device >> 2) & 1


def relative_places(place):
    x, y, core, z, far = device_bits()
    mirrored = (place & 25) | ((place & 4) >> 1) | ((place & 2) << 1)
    plain = jnp.where((place & 8) == 0, place, mirrored)
    return plain ^ (core * 16 + far * 8 + x * 4 + y * 2 + z)


def edge_order():
    return relative_places(jnp.arange(CHUNKS, dtype=jnp.int32))


def node_order():
    place = jnp.arange(CHUNKS, dtype=jnp.int32)
    return relative_places(((place & 4) << 2) | ((place & 24) >> 1) | (place & 3))


def shape(*dims, kind=F32):
    return jax.ShapeDtypeStruct(dims, kind)


def params(mebibytes):
    return pltpu.CompilerParams(vmem_limit_bytes=mebibytes << 20)


def whole(*dims):
    return pl.BlockSpec(dims, lambda *_: (0,) * len(dims), pipeline_mode=pl.Buffered(1))


def result(*dims):
    return pl.BlockSpec(dims, lambda *_: (0,) * len(dims))


def per_device(
    node_latent,
    edge_latent,
    node_cotangent,
    edge_cotangent,
    edge_sender,
    edge_receiver,
    live_counts,
    edge_lift,
    edge_bias,
    edge_mix,
    edge_gain,
    node_lift,
    node_bias,
    node_mix,
    node_gain,
):
    width = node_latent.shape[2]
    nodes = node_latent[0]
    count = nodes.shape[0]
    peers = edge_receiver.shape[1]
    slots = edge_receiver.shape[2]
    total_rows = peers * slots
    unit = total_rows * width * width
    edges = edge_latent.reshape(peers, slots, width)
    edge_seed = edge_cotangent.reshape(peers, slots, width)
    receivers = edge_receiver.reshape(peers, slots)
    live = live_counts.reshape(peers)
    mine = lax.axis_index("dev")
    paired = lax.axis_size("dev") == 8 and lax.axis_size("grp") == 4
    packed_rows = count + -(-peers // 16) * 16
    packed_nodes = pl.pallas_call(
        pack_kernel,
        out_shape=shape(packed_rows, width, kind=BF16),
        compiler_params=params(4),
        name="pack",
    )(nodes, edge_sender)
    if paired:
        owners = jnp.arange(peers, dtype=jnp.int32) ^ mine
        edge_places = edge_order()
        node_places = node_order()
        near = swap(packed_nodes, "dev", 2)
        across = swap(packed_nodes, "dev", 4)
        beside, across = lax.optimization_barrier((swap(packed_nodes, "dev", 1), across))
        far = [near, across, swap(across, "dev", 2)]
        pieces = [packed_nodes, beside]
        pieces = [piece[None] for piece in pieces]
        ranges = [(0, 2), (2, 8)]
    else:
        owners = jnp.arange(peers, dtype=jnp.int32)
        edge_places = node_places = jnp.arange(CHUNKS, dtype=jnp.int32)
        pieces = [lax.all_gather(packed_nodes, "dev")]
        ranges = [(0, peers)]
    gathered_rows = pieces[0].shape[1]

    anywhere = pl.BlockSpec(memory_space=pl.ANY)
    bias_row = edge_bias.reshape(1, width)
    gain_row = edge_gain.reshape(1, width)

    owned = pl.BlockSpec((1, slots, width), lambda i: (i, 0, 0))
    pre = pl.pallas_call(
        lift_kernel,
        grid=(peers,),
        in_specs=[
            owned,
            whole(peers, slots),
            whole(count, width),
            whole(3 * width, width),
            whole(1, width),
        ],
        out_specs=owned,
        out_shape=shape(peers, slots, width),
        compiler_params=params(12),
        cost_estimate=pl.CostEstimate(
            flops=5 * unit, bytes_accessed=6 * total_rows * width, transcendentals=0
        ),
        name="lift",
    )(edges, receivers, nodes, edge_lift, bias_row)

    def by_owner(*dims):
        return pl.BlockSpec(
            (1,) + dims, lambda i, owner, *_: (owner[i],) + (0,) * len(dims)
        )

    def by_step(*dims):
        return pl.BlockSpec((1,) + dims, lambda i, *_: (i,) + (0,) * len(dims))

    saved = []
    summed = None
    for begin, end in ranges:
        first, last = begin == 0, end == peers
        if not first:
            *far, summed = lax.optimization_barrier((*far, summed))
            for piece in far:
                pieces += [piece[None], swap(piece, "dev", 1)[None]]
        chosen = pieces[begin:] if paired else pieces

        def saved_step(*dims, begin=begin):
            return pl.BlockSpec((1,) + dims, lambda i, *_: (i + begin,) + (0,) * len(dims))

        operands = chosen + [
            pre,
            receivers,
            nodes,
            edge_lift,
            edge_mix,
            gain_row,
        ]
        in_specs = [anywhere] * len(chosen) + [
            by_owner(slots, width),
            whole(peers, slots),
            whole(count, width),
            pl.BlockSpec((width, width), lambda *_: (1, 0), pipeline_mode=pl.Buffered(1)),
            whole(width, width),
            whole(1, width),
        ]
        aliases = {}
        if not first:
            aliases = {4 + len(operands) + j: j for j in range(4)}
            operands += saved + [summed]
            in_specs += [anywhere] * 4 + [whole(count, width)]
        out_specs = [saved_step(slots, width)] * 3 + [saved_step(slots, 1)]
        out_shape = [shape(peers, slots, width, kind=BF16)] * 3 + [shape(peers, slots, 1)]
        scratch = [
            pltpu.VMEM((end - begin, gathered_rows, width), BF16),
            pltpu.SemaphoreType.DMA((len(chosen),)),
        ]
        if last:
            operands += [
                node_cotangent[0],
                node_lift,
                node_bias.reshape(1, width),
                node_mix,
                node_gain.reshape(1, width),
            ]
            in_specs += [whole(count, width), anywhere, whole(1, width), anywhere, whole(1, width)]
            out_specs += [
                result(count, width),
                result(count, width),
                result(3 * width, width),
                result(2, width),
            ]
            out_shape += [
                shape(count, width),
                shape(count, width, kind=BF16),
                shape(3 * width, width, kind=BF16),
                shape(2, width),
            ]
            scratch += [
                pltpu.VMEM((count, width), F32),
                pltpu.VMEM((3 * width, width), F32),
                pltpu.VMEM((2 * width, width), BF16),
                pltpu.VMEM((width, width), BF16),
                pltpu.SemaphoreType.DMA((2,)),
            ]
        else:
            out_specs.append(result(count, width))
            out_shape.append(shape(count, width))
        results = pl.pallas_call(
            functools.partial(forward_kernel, len(chosen), first, last),
            grid_spec=pltpu.PrefetchScalarGridSpec(
                num_scalar_prefetch=4,
                grid=(end - begin,),
                in_specs=in_specs,
                out_specs=out_specs,
                scratch_shapes=scratch,
            ),
            out_shape=out_shape,
            input_output_aliases=aliases,
            compiler_params=params(24),
            cost_estimate=pl.CostEstimate(
                flops=4 * unit,
                bytes_accessed=8 * total_rows * width,
                transcendentals=total_rows * width,
            ),
            name="forward_" + ("all" if last else "near"),
        )(owners[begin:end], live, node_places, mine.reshape(1), *operands)
        saved = list(results[:4])
        if last:
            base, summed_grad, node_packed, node_small = results[4:]
        else:
            summed = results[4]
    hidden, normed, slope, inverse = saved

    if paired:
        node_kept, node_got = node_start(node_packed)
    grad_edges, partial, grad_nodes, edge_packed, edge_small = pl.pallas_call(
        functools.partial(backward_kernel, len(pieces)),
        grid_spec=pltpu.PrefetchScalarGridSpec(
            num_scalar_prefetch=4,
            grid=(peers,),
            in_specs=[anywhere] * len(pieces)
            + [
                by_owner(slots, width),
                by_owner(slots, width),
                whole(peers, slots),
                by_step(slots, width),
                by_step(slots, width),
                by_step(slots, width),
                by_step(slots, 1),
                whole(count, width),
                whole(count, width),
                whole(count, width),
                whole(3 * width, width),
                whole(width, width),
                whole(1, width),
            ],
            out_specs=[
                by_owner(slots, width),
                pl.BlockSpec((1, 1, count, width), lambda i, *_: (i % 2, i // 2, 0, 0)),
                result(count, width),
                result(4 * width, width),
                result(2, width),
            ],
            scratch_shapes=[
                pltpu.VMEM((count, width), F32),
                pltpu.VMEM((4 * width, width), F32),
                pltpu.VMEM((peers, gathered_rows, width), BF16),
                pltpu.SemaphoreType.DMA((len(pieces),)),
            ],
        ),
        out_shape=[
            shape(peers, slots, width, kind=BF16),
            shape(2, peers // 2, count, width, kind=BF16),
            shape(count, width),
            shape(4 * width, width, kind=BF16),
            shape(2, width),
        ],
        compiler_params=params(28),
        cost_estimate=pl.CostEstimate(
            flops=14 * unit, bytes_accessed=20 * total_rows * width, transcendentals=0
        ),
        name="backward",
    )(
        owners,
        live,
        edge_places,
        mine.reshape(1),
        *pieces,
        edges,
        edge_seed,
        receivers,
        hidden,
        normed,
        slope,
        inverse,
        nodes,
        base,
        summed_grad,
        edge_lift,
        edge_mix,
        gain_row,
    )

    if paired:
        edge_packed, edge_small, *node_got = lax.optimization_barrier(
            (edge_packed, edge_small, *node_got)
        )
    small = jnp.concatenate([edge_small, node_small])
    if paired:
        sources, small, from_senders = reduce_all(
            edge_packed, node_kept, node_got, partial, small
        )
    else:
        node_sum, edge_sum, small = lax.psum(
            (node_packed.astype(F32), edge_packed.astype(F32), small), ("grp", "dev")
        )
        interleaved = jnp.concatenate(
            [
                edge_sum.reshape(CHUNKS, 4 * width // CHUNKS, width),
                node_sum.reshape(CHUNKS, 3 * width // CHUNKS, width),
            ],
            axis=1,
        )
        sources = [[(interleaved.reshape(7 * width, width).astype(BF16), 0)]]
        ordered = jnp.swapaxes(partial, 0, 1).reshape(peers, count, width)
        from_senders = lax.psum_scatter(ordered.astype(F32), "dev", scatter_dimension=0)
    grad_nodes = grad_nodes + contract_features(
        from_senders.astype(BF16), edge_lift[width : 2 * width]
    )
    groups = lax.axis_size("grp") * lax.axis_size("dev")
    edge_scale = float(total_rows * groups) ** (-0.5)
    node_scale = float(count * groups) ** (-0.5)
    totals = [3 * width, width, 2 * width, width]
    unpacked = []
    for part in sources:
        part, starts = zip(*part)
        places = sum(source.shape[0] for source in part) * CHUNKS // (7 * width)
        unpacked = pl.pallas_call(
            functools.partial(unpack_kernel, (edge_scale, node_scale), starts),
            grid_spec=pltpu.PrefetchScalarGridSpec(
                num_scalar_prefetch=1,
                grid=(1,),
                in_specs=[whole(*source.shape) for source in part] + [anywhere] * len(unpacked),
                out_specs=[anywhere] * 4,
                scratch_shapes=[
                    pltpu.VMEM((places * total // CHUNKS, width), F32) for total in totals
                ]
                + [pltpu.SemaphoreType.DMA((4, places))],
            ),
            out_shape=[shape(total, width) for total in totals],
            input_output_aliases={1 + len(part) + j: j for j in range(len(unpacked))},
            compiler_params=params(20),
            cost_estimate=pl.CostEstimate(
                flops=0, bytes_accessed=42 * places * width * width // CHUNKS, transcendentals=0
            ),
            name="unpack_%d" % starts[0],
        )(edge_places, *part, *unpacked)
    edge_lift_grad, edge_mix_grad, node_lift_grad, node_mix_grad = unpacked
    return (
        grad_nodes[None],
        grad_edges.reshape(1, 1, peers, slots, width),
        edge_lift_grad,
        small[0] * edge_scale,
        edge_mix_grad,
        small[1] * edge_scale,
        node_lift_grad,
        small[2] * node_scale,
        node_mix_grad,
        small[3] * node_scale,
    )


def solution(mesh):
    return jax.shard_map(
        per_device,
        mesh=mesh,
        in_specs=(
            P("grp", "dev", None),
            P("grp", "dev", None, None, None),
            P("grp", "dev", None),
            P("grp", "dev", None, None, None),
            P(None, "dev", None),
            P("dev", None, None),
            P("dev", None),
            P(),
            P(),
            P(),
            P(),
            P(),
            P(),
            P(),
            P(),
        ),
        out_specs=(
            P("grp", "dev", None),
            P("grp", "dev", None, None, None),
            P(),
            P(),
            P(),
            P(),
            P(),
            P(),
            P(),
            P(),
        ),
        check_vma=False,
    )
```

```python
import functools

import jax
import jax.numpy as jnp
from jax import lax
from jax.experimental import pallas as pl
from jax.experimental.pallas import tpu as pltpu
from jax.sharding import PartitionSpec as P

EPSILON = 1e-05
CHUNKS = 32
BF16 = jnp.bfloat16
F32 = jnp.float32


def matmul(left, right):
    return jnp.dot(left, right, preferred_element_type=F32)


def contract_rows(left, right):
    return lax.dot_general(left, right, (((0,), (0,)), ((), ())), preferred_element_type=F32)


def contract_features(left, right):
    return lax.dot_general(left, right, (((1,), (1,)), ((), ())), preferred_element_type=F32)


def one_hot(index_row, nodes):
    rows = lax.broadcasted_iota(jnp.int32, (nodes, index_row.shape[1]), 0)
    return jnp.where(rows == index_row, 1.0, 0.0).astype(BF16)


def silu_pair(values):
    gate = 0.5 * jnp.tanh(0.5 * values) + 0.5
    hidden = values * gate
    return hidden, gate + hidden * (1.0 - gate)


def norm_forward(values):
    centred = values - jnp.mean(values, axis=-1, keepdims=True)
    inverse = lax.rsqrt(jnp.mean(centred * centred, axis=-1, keepdims=True) + EPSILON)
    return centred * inverse, inverse


def norm_backward(grad_hat, normed, inverse):
    spread = jnp.mean(grad_hat * normed, axis=-1, keepdims=True)
    return inverse * (grad_hat - jnp.mean(grad_hat, axis=-1, keepdims=True) - normed * spread)


def pick_row(block, place):
    rows = lax.broadcasted_iota(jnp.int32, block.shape, 0)
    picked = jnp.sum(jnp.where(rows == place, block.astype(F32), 0.0), axis=0, keepdims=True)
    return picked.astype(jnp.int32)


def pack_kernel(nodes_ref, sender_ref, packed_ref):
    count, width = nodes_ref.shape
    peers, _, slots = sender_ref.shape
    packed_ref[:count] = nodes_ref[...]
    packed_ref[count:] = jnp.zeros((packed_ref.shape[0] - count, width), BF16)
    packed_ref[count : count + peers, :slots] = sender_ref[:, 0, :].astype(F32).astype(BF16)


def live_rows(count, shape):
    return lax.broadcasted_iota(jnp.int32, shape, 0) < count


def store_chunks(order_ref, source_ref, target_ref, mix_rows):
    mix_part = mix_rows // CHUNKS
    rows = source_ref.shape[0] // CHUNKS
    lift_part = rows - mix_part
    lift_rows = lift_part * CHUNKS

    def step(place, carry):
        chunk = order_ref[place]
        target = pl.multiple_of(place * rows, 16)
        lift_start = pl.multiple_of(chunk * lift_part, 16)
        mix_start = pl.multiple_of(lift_rows + chunk * mix_part, 16)
        target_ref[pl.ds(target, lift_part), :] = source_ref[
            pl.ds(lift_start, lift_part), :
        ].astype(BF16)
        target_ref[pl.ds(pl.multiple_of(target + lift_part, 16), mix_part), :] = source_ref[
            pl.ds(mix_start, mix_part), :
        ].astype(BF16)
        return carry

    lax.fori_loop(0, CHUNKS, step, 0)


def lift_kernel(edges_ref, receiver_ref, nodes_ref, lift_ref, bias_ref, pre_ref):
    width = nodes_ref.shape[1]
    table = one_hot(receiver_ref[pl.ds(pl.program_id(0), 1), :], nodes_ref.shape[0])
    receivers = contract_rows(table, nodes_ref[...]).astype(BF16)
    pre_ref[0] = (
        matmul(edges_ref[0], lift_ref[:width])
        + matmul(receivers, lift_ref[2 * width :])
        + bias_ref[...]
    )


def by_live(count, slots, body):
    part = slots // 4
    for quarter in range(1, 5):
        low = (quarter - 1) * part if quarter > 1 else -1

        @pl.when((count > low) & (count <= quarter * part))
        def _(rows=quarter * part):
            body(rows)


def load_pieces(step, sources, held_ref, sems):
    copies, start = [], 0
    for place, source in enumerate(sources):
        size = source.shape[0]
        copies.append(
            (start, pltpu.make_async_copy(source, held_ref.at[pl.ds(start, size)], sems.at[place]))
        )
        start += size

    @pl.when(step == 0)
    def _():
        for _, copy in copies:
            copy.start()

    for first, copy in copies:

        @pl.when(step == first)
        def _(copy=copy):
            copy.wait()


def forward_kernel(pieces, first, last, *refs):
    refs = list(refs)
    take = lambda size: [refs.pop(0) for _ in range(size)]
    owner_ref, live_ref, order_ref, mine_ref = take(4)
    sources = take(pieces)
    pre_ref, receiver_ref, nodes_ref, lift_ref, mix_ref, gain_ref = take(6)
    if not first:
        take(4)
        (carried_ref,) = take(1)
    if last:
        seed_ref, node_lift_hbm, node_bias_ref, node_mix_hbm, node_gain_ref = take(5)
    hidden_ref, normed_ref, slope_ref, inverse_ref = take(4)
    if last:
        base_ref, summed_grad_ref, packed_ref, small_ref = take(4)
    else:
        (summed_ref,) = take(1)
    held_ref, sems = take(2)
    if last:
        summed_ref, total_ref, node_lift_ref, node_mix_ref, weight_sems = take(5)
    step = pl.program_id(0)
    count, width = nodes_ref.shape
    load_pieces(step, sources, held_ref, sems)
    if last:
        loads = [
            pltpu.make_async_copy(node_lift_hbm, node_lift_ref, weight_sems.at[0]),
            pltpu.make_async_copy(node_mix_hbm, node_mix_ref, weight_sems.at[1]),
        ]

    @pl.when(step == 0)
    def _():
        if last:
            for load in loads:
                load.start()
        summed_ref[...] = jnp.zeros_like(summed_ref) if first else carried_ref[...]

    owner = owner_ref[step]
    live_count = live_ref[owner]
    slots = pre_ref.shape[1]

    def body(rows):
        index = pick_row(held_ref[step, count:, :rows], mine_ref[0])
        senders = contract_rows(one_hot(index, count), held_ref[step, :count]).astype(BF16)
        pre = pre_ref[0, :rows] + matmul(senders, lift_ref[...])
        hidden, slope = silu_pair(pre)
        hidden = hidden.astype(BF16)
        normed, inverse = norm_forward(matmul(hidden, mix_ref[...]))
        hidden_ref[0, :rows] = hidden
        slope_ref[0, :rows] = slope.astype(BF16)
        normed_ref[0, :rows] = normed.astype(BF16)
        inverse_ref[0, :rows] = inverse
        if rows < slots:
            for saved_ref in (hidden_ref, slope_ref, normed_ref, inverse_ref):
                saved_ref[0, rows:] = jnp.zeros_like(saved_ref[0, rows:])
        live = live_rows(live_count, normed.shape)
        message = jnp.where(live, normed * gain_ref[...], 0.0).astype(BF16)
        summed_ref[...] += matmul(one_hot(receiver_ref[pl.ds(owner, 1), :][:, :rows], count), message)

    by_live(live_count, slots, body)

    if not last:
        return

    @pl.when(step == pl.num_programs(0) - 1)
    def _():
        for load in loads:
            load.wait()
        nodes = nodes_ref[...]
        summed = summed_ref[...].astype(BF16)
        pre_node = (
            matmul(nodes, node_lift_ref[:width])
            + matmul(summed, node_lift_ref[width:])
            + node_bias_ref[...]
        )
        hidden_node, slope_node = silu_pair(pre_node)
        hidden_node = hidden_node.astype(BF16)
        normed_node, inverse_node = norm_forward(matmul(hidden_node, node_mix_ref[...]))
        seed = seed_ref[...].astype(F32)
        small_ref[1:2, :] = jnp.sum(seed * normed_node, axis=0, keepdims=True)
        grad_out = norm_backward(seed * node_gain_ref[...], normed_node, inverse_node).astype(BF16)
        total_ref[2 * width :, :] = contract_rows(hidden_node, grad_out)
        grad_pre = (contract_features(grad_out, node_mix_ref[...]) * slope_node).astype(BF16)
        small_ref[0:1, :] = jnp.sum(grad_pre.astype(F32), axis=0, keepdims=True)
        total_ref[:width, :] = contract_rows(nodes, grad_pre)
        total_ref[width : 2 * width, :] = contract_rows(summed, grad_pre)
        base_ref[...] = seed + contract_features(grad_pre, node_lift_ref[:width])
        summed_grad_ref[...] = contract_features(grad_pre, node_lift_ref[width:]).astype(BF16)
        store_chunks(order_ref, total_ref, packed_ref, width)


def backward_kernel(pieces, *refs):
    arrival_ref, live_ref, order_ref, mine_ref = refs[:4]
    sources = refs[4 : 4 + pieces]
    (
        edges_ref,
        seed_ref,
        receiver_ref,
        hidden_ref,
        normed_ref,
        slope_ref,
        inverse_ref,
        nodes_ref,
        base_ref,
        summed_grad_ref,
        lift_ref,
        mix_ref,
        gain_ref,
        grad_edges_ref,
        partial_ref,
        grad_nodes_ref,
        packed_ref,
        small_ref,
        received_ref,
        total_ref,
        held_ref,
        out_ref,
        pre_ref,
        sent_ref,
        sems,
    ) = refs[4 + pieces :]
    step = pl.program_id(0)
    count, width = nodes_ref.shape
    group, slots = edges_ref.shape[:2]
    rows = group * slots
    copies, start = [], 0
    for place, source in enumerate(sources):
        size = source.shape[0]
        copies.append(
            pltpu.make_async_copy(source, held_ref.at[pl.ds(start, size)], sems.at[place])
        )
        start += size

    @pl.when(step == 0)
    def _():
        for copy in copies:
            copy.start()
        received_ref[...] = jnp.zeros_like(received_ref)
        total_ref[...] = jnp.zeros_like(total_ref)
        small_ref[...] = jnp.zeros_like(small_ref)

    tables = []
    for member in range(group):
        owner = step * group + member
        seed = seed_ref[member].astype(F32)
        live = live_rows(live_ref[owner], seed.shape)
        table = one_hot(receiver_ref[pl.ds(owner, 1), :], count)
        tables.append(table)
        grad_message = jnp.where(
            live, seed + contract_rows(table, summed_grad_ref[...]), 0.0
        )
        normed = normed_ref[member].astype(F32)
        small_ref[1:2, :] += jnp.sum(grad_message * normed, axis=0, keepdims=True)
        grad_out = norm_backward(
            grad_message * gain_ref[...], normed, inverse_ref[member]
        ).astype(BF16)
        grad_pre = (
            contract_features(grad_out, mix_ref[...]) * slope_ref[member].astype(F32)
        ).astype(BF16)
        out_ref[member * slots : (member + 1) * slots, :] = grad_out
        pre_ref[member * slots : (member + 1) * slots, :] = grad_pre
        small_ref[0:1, :] += jnp.sum(grad_pre.astype(F32), axis=0, keepdims=True)
        grad_edges_ref[member] = jnp.where(
            live, seed + contract_features(grad_pre, lift_ref[:width]), 0.0
        ).astype(BF16)

    @pl.when(step == 0)
    def _():
        for copy in copies:
            copy.wait()

    first_arrival = (arrival_ref[step * group] // group) * group
    for member in range(group):
        arrival = arrival_ref[step * group + member]
        place = arrival - first_arrival
        index = pick_row(held_ref[arrival, count:, :slots], mine_ref[0])
        sent = matmul(
            one_hot(index, count), pre_ref[member * slots : (member + 1) * slots, :]
        ).astype(BF16)
        partial_ref[place % 2, place // 2] = sent
        sent_ref[place] = sent
    received_ref[...] += matmul(jnp.concatenate(tables, axis=1), pre_ref[...])
    total_ref[3 * width :, :] += contract_rows(
        hidden_ref[...].reshape(rows, width), out_ref[...]
    )
    total_ref[:width, :] += contract_rows(edges_ref[...].reshape(rows, width), pre_ref[...])
    total_ref[width : 2 * width, :] += contract_rows(
        held_ref[pl.ds(first_arrival, group), :count].reshape(group * count, width),
        sent_ref[...].reshape(group * count, width),
    )

    @pl.when(step == pl.num_programs(0) - 1)
    def _():
        received = received_ref[...].astype(BF16)
        total_ref[2 * width : 3 * width, :] = contract_rows(nodes_ref[...], received)
        grad_nodes_ref[...] = base_ref[...] + contract_features(received, lift_ref[2 * width :])
        store_chunks(order_ref, total_ref, packed_ref, width)


def unpack_kernel(scale, places, *refs):
    order_ref = refs[0]
    sources = refs[1 : 1 + len(places)]
    targets = refs[-9:-5]
    buffers = refs[-5:-1]
    sems = refs[-1]
    parts = [target.shape[0] // CHUNKS for target in targets]
    copies, slot = [], 0
    for source, place in zip(sources, places):
        for start in range(0, source.shape[0], sum(parts)):
            for kind, rows in enumerate(parts):
                held = buffers[kind].at[pl.ds(slot * rows, rows)]
                held[...] = source[start : start + rows, :].astype(F32) * scale[kind // 2]
                target = pl.multiple_of(order_ref[place] * rows, 16)
                copies.append(
                    pltpu.make_async_copy(
                        held, targets[kind].at[pl.ds(target, rows)], sems.at[kind, slot]
                    )
                )
                copies[-1].start()
                start += rows
            slot += 1
            place += 1
    for copy in copies:
        copy.wait()


def swap(values, axis, bit):
    size = lax.axis_size(axis)
    return lax.ppermute(values, axis, [(i, i ^ bit) for i in range(size)])


def add_rounded(left, right):
    return (left.astype(F32) + right.astype(F32)).astype(BF16)


def exchange(*moves):
    values = lax.optimization_barrier(tuple(move[0] for move in moves))
    moved = [swap(value, axis, bit) for value, (_, axis, bit) in zip(values, moves)]
    return lax.optimization_barrier(tuple(moved))


def halves(part):
    rows = part.shape[0] // 2
    return part[:rows], part[rows:]


def halves_inner(blocks):
    rows = blocks.shape[1] // 2
    return blocks[:, :rows], blocks[:, rows:]


def join(*parts):
    return jnp.concatenate(parts)


def node_start(node_packed):
    sides = [halves(side) for side in halves(node_packed)]
    got = [swap(sides[0][1], "grp", 1), swap(sides[1][1], "grp", 2)]
    return [side[0] for side in sides], got


def reduce_all(edge_packed, node_kept, node_got, partial, small):
    node_a, node_b = [add_rounded(kept, got) for kept, got in zip(node_kept, node_got)]

    keep, send = halves(edge_packed)
    got, got_small, got_partial = exchange(
        (send, "dev", 1), (small, "dev", 1), (partial[1], "dev", 1)
    )
    edge_a, edge_b = halves(add_rounded(keep, got))
    small = small + got_small
    owned = add_rounded(partial[0], got_partial)
    owned_early, owned_late = halves_inner(owned)

    keep_a, send_a = halves(edge_a)
    keep_b, send_b = halves(edge_b)
    node_keep_a, node_send_a = halves(node_a)
    node_keep_b, node_send_b = halves(node_b)
    got_a, got_b, got_node, got_small, got_owned = exchange(
        (send_a, "grp", 1),
        (send_b, "grp", 2),
        (join(node_send_a, node_send_b), "dev", 1),
        (small, "grp", 1),
        (owned_early[1::2], "dev", 2),
    )
    edge_a, edge_b = add_rounded(keep_a, got_a), add_rounded(keep_b, got_b)
    got_node_a, got_node_b = halves(got_node)
    node_a, node_b = add_rounded(node_keep_a, got_node_a), add_rounded(node_keep_b, got_node_b)
    small = small + got_small
    owned_early = add_rounded(owned_early[::2], got_owned)

    pairs = [halves(part) for part in (edge_a, node_a, edge_b, node_b)]
    got_a, got_b, got_small, got_owned, got_early = exchange(
        (join(pairs[0][1], pairs[1][1]), "grp", 2),
        (join(pairs[2][1], pairs[3][1]), "grp", 1),
        (small, "grp", 2),
        (owned_late[1::2], "dev", 2),
        (owned_early[1], "dev", 4),
    )
    small = small + got_small
    owned_late = add_rounded(owned_late[::2], got_owned)
    edge_rows = pairs[0][0].shape[0]
    parts = [
        halves(add_rounded(pairs[0][0], got_a[:edge_rows])),
        halves(add_rounded(pairs[1][0], got_a[edge_rows:])),
        halves(add_rounded(pairs[2][0], got_b[:edge_rows])),
        halves(add_rounded(pairs[3][0], got_b[edge_rows:])),
    ]
    got_1, got_2, got_3, got_small = exchange(
        (join(parts[0][1], parts[1][1]), "dev", 2),
        (join(parts[2][0], parts[3][0]), "dev", 4),
        (join(parts[2][1], parts[3][1]), "dev", 6),
        (small, "dev", 2),
    )
    small = small + got_small
    kept = sum(
        (got.astype(F32) for got in (got_1, got_2, got_3)),
        join(parts[0][0], parts[1][0]).astype(F32),
    ).astype(BF16)
    got_1, got_2, got_small = exchange((kept, "dev", 2), (kept, "dev", 4), (small, "dev", 4))
    (got_3,) = exchange((got_2, "dev", 2))
    small = small + got_small

    side_a, side_b = join(kept, got_1), join(got_2, got_3)
    got_a, got_b, got_late = exchange(
        (side_a, "grp", 2), (side_b, "grp", 1), (owned_late[1], "dev", 4)
    )
    from_senders = join(owned_early[0], owned_late[0]).astype(F32) + join(
        got_early, got_late
    ).astype(F32)
    side_a, side_b = join(side_a, got_a), join(side_b, got_b)
    got_a, got_b, swapped_a, swapped_b = exchange(
        (side_a, "grp", 1),
        (side_b, "grp", 2),
        (side_a, "dev", 1),
        (side_b, "dev", 1),
    )
    last_a, last_b = exchange((got_a, "dev", 1), (got_b, "dev", 1))
    sources = [
        [(side_a, 0), (side_b, 8)],
        [
            (got_a, 4),
            (got_b, 12),
            (swapped_a, 16),
            (swapped_b, 24),
            (last_a, 20),
            (last_b, 28),
        ],
    ]
    return sources, small, from_senders


def device_bits():
    group = lax.axis_index("grp")
    device = lax.axis_index("dev")
    return group & 1, group >> 1, device & 1, (device >> 1) & 1, (device >> 2) & 1


def relative_places(place):
    x, y, core, z, far = device_bits()
    mirrored = (place & 25) | ((place & 4) >> 1) | ((place & 2) << 1)
    plain = jnp.where((place & 8) == 0, place, mirrored)
    return plain ^ (core * 16 + far * 8 + x * 4 + y * 2 + z)


def edge_order():
    return relative_places(jnp.arange(CHUNKS, dtype=jnp.int32))


def node_order():
    place = jnp.arange(CHUNKS, dtype=jnp.int32)
    return relative_places(((place & 4) << 2) | ((place & 24) >> 1) | (place & 3))


def shape(*dims, kind=F32):
    return jax.ShapeDtypeStruct(dims, kind)


def params(mebibytes):
    return pltpu.CompilerParams(vmem_limit_bytes=mebibytes << 20)


def whole(*dims):
    return pl.BlockSpec(dims, lambda *_: (0,) * len(dims), pipeline_mode=pl.Buffered(1))


def result(*dims):
    return pl.BlockSpec(dims, lambda *_: (0,) * len(dims))


def per_device(
    node_latent,
    edge_latent,
    node_cotangent,
    edge_cotangent,
    edge_sender,
    edge_receiver,
    live_counts,
    edge_lift,
    edge_bias,
    edge_mix,
    edge_gain,
    node_lift,
    node_bias,
    node_mix,
    node_gain,
):
    width = node_latent.shape[2]
    nodes = node_latent[0]
    count = nodes.shape[0]
    peers = edge_receiver.shape[1]
    slots = edge_receiver.shape[2]
    total_rows = peers * slots
    unit = total_rows * width * width
    edges = edge_latent.reshape(peers, slots, width)
    edge_seed = edge_cotangent.reshape(peers, slots, width)
    receivers = edge_receiver.reshape(peers, slots)
    live = live_counts.reshape(peers)
    mine = lax.axis_index("dev")
    paired = lax.axis_size("dev") == 8 and lax.axis_size("grp") == 4
    packed_rows = count + -(-peers // 16) * 16
    packed_nodes = pl.pallas_call(
        pack_kernel,
        out_shape=shape(packed_rows, width, kind=BF16),
        compiler_params=params(4),
        name="pack",
    )(nodes, edge_sender)
    if paired:
        owners = jnp.arange(peers, dtype=jnp.int32) ^ mine
        edge_places = edge_order()
        node_places = node_order()
        near = swap(packed_nodes, "dev", 2)
        across = swap(packed_nodes, "dev", 4)
        beside, across = lax.optimization_barrier((swap(packed_nodes, "dev", 1), across))
        behind = swap(across, "dev", 2)
        pieces = [packed_nodes, beside]
        pieces = [piece[None] for piece in pieces]
        ranges = [(0, 2), (2, 6), (6, 8)]
    else:
        owners = jnp.arange(peers, dtype=jnp.int32)
        edge_places = node_places = jnp.arange(CHUNKS, dtype=jnp.int32)
        pieces = [lax.all_gather(packed_nodes, "dev")]
        ranges = [(0, peers)]
    gathered_rows = pieces[0].shape[1]

    anywhere = pl.BlockSpec(memory_space=pl.ANY)
    bias_row = edge_bias.reshape(1, width)
    gain_row = edge_gain.reshape(1, width)

    owned = pl.BlockSpec((1, slots, width), lambda i: (i, 0, 0))
    pre = pl.pallas_call(
        lift_kernel,
        grid=(peers,),
        in_specs=[
            owned,
            whole(peers, slots),
            whole(count, width),
            whole(3 * width, width),
            whole(1, width),
        ],
        out_specs=owned,
        out_shape=shape(peers, slots, width),
        compiler_params=params(12),
        cost_estimate=pl.CostEstimate(
            flops=5 * unit, bytes_accessed=6 * total_rows * width, transcendentals=0
        ),
        name="lift",
    )(edges, receivers, nodes, edge_lift, bias_row)

    def by_owner(*dims):
        return pl.BlockSpec(
            (1,) + dims, lambda i, owner, *_: (owner[i],) + (0,) * len(dims)
        )

    group = 2

    def grouped(*dims):
        return pl.BlockSpec((group,) + dims, lambda i, *_: (i,) + (0,) * len(dims))

    saved = []
    summed = None
    for begin, end in ranges:
        first, last = begin == 0, end == peers
        if last and not first:
            behind, summed = lax.optimization_barrier((behind, summed))
        if not first:
            for piece in [behind] if last else [near, across]:
                pieces += [piece[None], swap(piece, "dev", 1)[None]]
        chosen = pieces[begin:] if paired else pieces

        operands = chosen + [
            pre,
            receivers,
            nodes,
            edge_lift,
            edge_mix,
            gain_row,
        ]
        in_specs = [anywhere] * len(chosen) + [
            by_owner(slots, width),
            whole(peers, slots),
            whole(count, width),
            pl.BlockSpec((width, width), lambda *_: (1, 0), pipeline_mode=pl.Buffered(1)),
            whole(width, width),
            whole(1, width),
        ]
        aliases = {}
        if not first:
            aliases = {4 + len(operands) + j: j for j in range(4)}
            operands += saved + [summed]
            in_specs += [anywhere] * 4 + [whole(count, width)]
        out_specs = [by_owner(slots, width)] * 3 + [by_owner(slots, 1)]
        out_shape = [shape(peers, slots, width, kind=BF16)] * 3 + [shape(peers, slots, 1)]
        scratch = [
            pltpu.VMEM((end - begin, gathered_rows, width), BF16),
            pltpu.SemaphoreType.DMA((len(chosen),)),
        ]
        if last:
            operands += [
                node_cotangent[0],
                node_lift,
                node_bias.reshape(1, width),
                node_mix,
                node_gain.reshape(1, width),
            ]
            in_specs += [whole(count, width), anywhere, whole(1, width), anywhere, whole(1, width)]
            out_specs += [
                result(count, width),
                result(count, width),
                result(3 * width, width),
                result(2, width),
            ]
            out_shape += [
                shape(count, width),
                shape(count, width, kind=BF16),
                shape(3 * width, width, kind=BF16),
                shape(2, width),
            ]
            scratch += [
                pltpu.VMEM((count, width), F32),
                pltpu.VMEM((3 * width, width), F32),
                pltpu.VMEM((2 * width, width), BF16),
                pltpu.VMEM((width, width), BF16),
                pltpu.SemaphoreType.DMA((2,)),
            ]
        else:
            out_specs.append(result(count, width))
            out_shape.append(shape(count, width))
        results = pl.pallas_call(
            functools.partial(forward_kernel, len(chosen), first, last),
            grid_spec=pltpu.PrefetchScalarGridSpec(
                num_scalar_prefetch=4,
                grid=(end - begin,),
                in_specs=in_specs,
                out_specs=out_specs,
                scratch_shapes=scratch,
            ),
            out_shape=out_shape,
            input_output_aliases=aliases,
            compiler_params=params(24),
            cost_estimate=pl.CostEstimate(
                flops=4 * unit,
                bytes_accessed=8 * total_rows * width,
                transcendentals=total_rows * width,
            ),
            name="forward_%d" % begin,
        )(owners[begin:end], live, node_places, mine.reshape(1), *operands)
        saved = list(results[:4])
        if last:
            base, summed_grad, node_packed, node_small = results[4:]
        else:
            summed = results[4]
    hidden, normed, slope, inverse = saved

    if paired:
        node_kept, node_got = node_start(node_packed)
    grad_edges, partial, grad_nodes, edge_packed, edge_small = pl.pallas_call(
        functools.partial(backward_kernel, len(pieces)),
        grid_spec=pltpu.PrefetchScalarGridSpec(
            num_scalar_prefetch=4,
            grid=(peers // group,),
            in_specs=[anywhere] * len(pieces)
            + [
                grouped(slots, width),
                grouped(slots, width),
                whole(peers, slots),
                grouped(slots, width),
                grouped(slots, width),
                grouped(slots, width),
                grouped(slots, 1),
                whole(count, width),
                whole(count, width),
                whole(count, width),
                whole(3 * width, width),
                whole(width, width),
                whole(1, width),
            ],
            out_specs=[
                grouped(slots, width),
                pl.BlockSpec(
                    (2, group // 2, count, width),
                    lambda i, arrival, *_: (0, arrival[i * group] // group, 0, 0),
                ),
                result(count, width),
                result(4 * width, width),
                result(2, width),
            ],
            scratch_shapes=[
                pltpu.VMEM((count, width), F32),
                pltpu.VMEM((4 * width, width), F32),
                pltpu.VMEM((peers, gathered_rows, width), BF16),
                pltpu.VMEM((group * slots, width), BF16),
                pltpu.VMEM((group * slots, width), BF16),
                pltpu.VMEM((group, count, width), BF16),
                pltpu.SemaphoreType.DMA((len(pieces),)),
            ],
        ),
        out_shape=[
            shape(peers, slots, width, kind=BF16),
            shape(2, peers // 2, count, width, kind=BF16),
            shape(count, width),
            shape(4 * width, width, kind=BF16),
            shape(2, width),
        ],
        compiler_params=params(30),
        cost_estimate=pl.CostEstimate(
            flops=14 * unit, bytes_accessed=20 * total_rows * width, transcendentals=0
        ),
        name="backward",
    )(
        owners,
        live,
        edge_places,
        mine.reshape(1),
        *pieces,
        edges,
        edge_seed,
        receivers,
        hidden,
        normed,
        slope,
        inverse,
        nodes,
        base,
        summed_grad,
        edge_lift,
        edge_mix,
        gain_row,
    )

    if paired:
        edge_packed, edge_small, *node_got = lax.optimization_barrier(
            (edge_packed, edge_small, *node_got)
        )
    small = jnp.concatenate([edge_small, node_small])
    if paired:
        sources, small, from_senders = reduce_all(
            edge_packed, node_kept, node_got, partial, small
        )
    else:
        node_sum, edge_sum, small = lax.psum(
            (node_packed.astype(F32), edge_packed.astype(F32), small), ("grp", "dev")
        )
        interleaved = jnp.concatenate(
            [
                edge_sum.reshape(CHUNKS, 4 * width // CHUNKS, width),
                node_sum.reshape(CHUNKS, 3 * width // CHUNKS, width),
            ],
            axis=1,
        )
        sources = [[(interleaved.reshape(7 * width, width).astype(BF16), 0)]]
        ordered = jnp.swapaxes(partial, 0, 1).reshape(peers, count, width)
        from_senders = lax.psum_scatter(ordered.astype(F32), "dev", scatter_dimension=0)
    grad_nodes = grad_nodes + contract_features(
        from_senders.astype(BF16), edge_lift[width : 2 * width]
    )
    groups = lax.axis_size("grp") * lax.axis_size("dev")
    edge_scale = float(total_rows * groups) ** (-0.5)
    node_scale = float(count * groups) ** (-0.5)
    totals = [3 * width, width, 2 * width, width]
    unpacked = []
    for part in sources:
        part, starts = zip(*part)
        places = sum(source.shape[0] for source in part) * CHUNKS // (7 * width)
        unpacked = pl.pallas_call(
            functools.partial(unpack_kernel, (edge_scale, node_scale), starts),
            grid_spec=pltpu.PrefetchScalarGridSpec(
                num_scalar_prefetch=1,
                grid=(1,),
                in_specs=[whole(*source.shape) for source in part] + [anywhere] * len(unpacked),
                out_specs=[anywhere] * 4,
                scratch_shapes=[
                    pltpu.VMEM((places * total // CHUNKS, width), F32) for total in totals
                ]
                + [pltpu.SemaphoreType.DMA((4, places))],
            ),
            out_shape=[shape(total, width) for total in totals],
            input_output_aliases={1 + len(part) + j: j for j in range(len(unpacked))},
            compiler_params=params(20),
            cost_estimate=pl.CostEstimate(
                flops=0, bytes_accessed=42 * places * width * width // CHUNKS, transcendentals=0
            ),
            name="unpack_%d" % starts[0],
        )(edge_places, *part, *unpacked)
    edge_lift_grad, edge_mix_grad, node_lift_grad, node_mix_grad = unpacked
    return (
        grad_nodes[None],
        grad_edges.reshape(1, 1, peers, slots, width),
        edge_lift_grad,
        small[0] * edge_scale,
        edge_mix_grad,
        small[1] * edge_scale,
        node_lift_grad,
        small[2] * node_scale,
        node_mix_grad,
        small[3] * node_scale,
    )


def solution(mesh):
    return jax.shard_map(
        per_device,
        mesh=mesh,
        in_specs=(
            P("grp", "dev", None),
            P("grp", "dev", None, None, None),
            P("grp", "dev", None),
            P("grp", "dev", None, None, None),
            P(None, "dev", None),
            P("dev", None, None),
            P("dev", None),
            P(),
            P(),
            P(),
            P(),
            P(),
            P(),
            P(),
            P(),
        ),
        out_specs=(
            P("grp", "dev", None),
            P("grp", "dev", None, None, None),
            P(),
            P(),
            P(),
            P(),
            P(),
            P(),
            P(),
            P(),
        ),
        check_vma=False,
    )
```

```python
import functools

import jax
import jax.numpy as jnp
from jax import lax
from jax.experimental import pallas as pl
from jax.experimental.pallas import tpu as pltpu
from jax.sharding import PartitionSpec as P

EPSILON = 1e-05
CHUNKS = 32
BF16 = jnp.bfloat16
F32 = jnp.float32


def matmul(left, right):
    return jnp.dot(left, right, preferred_element_type=F32)


def contract_rows(left, right):
    return lax.dot_general(left, right, (((0,), (0,)), ((), ())), preferred_element_type=F32)


def contract_features(left, right):
    return lax.dot_general(left, right, (((1,), (1,)), ((), ())), preferred_element_type=F32)


def one_hot(index_row, nodes):
    rows = lax.broadcasted_iota(jnp.int32, (nodes, index_row.shape[1]), 0)
    return jnp.where(rows == index_row, 1.0, 0.0).astype(BF16)


def silu_pair(values):
    gate = 0.5 * jnp.tanh(0.5 * values) + 0.5
    hidden = values * gate
    return hidden, gate + hidden * (1.0 - gate)


def norm_forward(values):
    centred = values - jnp.mean(values, axis=-1, keepdims=True)
    inverse = lax.rsqrt(jnp.mean(centred * centred, axis=-1, keepdims=True) + EPSILON)
    return centred * inverse, inverse


def norm_backward(grad_hat, normed, inverse):
    spread = jnp.mean(grad_hat * normed, axis=-1, keepdims=True)
    return inverse * (grad_hat - jnp.mean(grad_hat, axis=-1, keepdims=True) - normed * spread)


def pick_row(block, place):
    rows = lax.broadcasted_iota(jnp.int32, block.shape, 0)
    picked = jnp.sum(jnp.where(rows == place, block.astype(F32), 0.0), axis=0, keepdims=True)
    return picked.astype(jnp.int32)


def pack_kernel(nodes_ref, sender_ref, packed_ref):
    count, width = nodes_ref.shape
    peers, _, slots = sender_ref.shape
    packed_ref[:count] = nodes_ref[...]
    packed_ref[count:] = jnp.zeros((packed_ref.shape[0] - count, width), BF16)
    packed_ref[count : count + peers, :slots] = sender_ref[:, 0, :].astype(F32).astype(BF16)


def live_rows(count, shape):
    return lax.broadcasted_iota(jnp.int32, shape, 0) < count


def store_chunks(order_ref, source_ref, target_ref, mix_rows):
    mix_part = mix_rows // CHUNKS
    rows = source_ref.shape[0] // CHUNKS
    lift_part = rows - mix_part
    lift_rows = lift_part * CHUNKS

    def step(place, carry):
        chunk = order_ref[place]
        target = pl.multiple_of(place * rows, 16)
        lift_start = pl.multiple_of(chunk * lift_part, 16)
        mix_start = pl.multiple_of(lift_rows + chunk * mix_part, 16)
        target_ref[pl.ds(target, lift_part), :] = source_ref[
            pl.ds(lift_start, lift_part), :
        ].astype(BF16)
        target_ref[pl.ds(pl.multiple_of(target + lift_part, 16), mix_part), :] = source_ref[
            pl.ds(mix_start, mix_part), :
        ].astype(BF16)
        return carry

    lax.fori_loop(0, CHUNKS, step, 0)


def lift_kernel(edges_ref, receiver_ref, nodes_ref, lift_ref, bias_ref, pre_ref):
    width = nodes_ref.shape[1]
    table = one_hot(receiver_ref[pl.ds(pl.program_id(0), 1), :], nodes_ref.shape[0])
    receivers = contract_rows(table, nodes_ref[...]).astype(BF16)
    pre_ref[0] = (
        matmul(edges_ref[0], lift_ref[:width])
        + matmul(receivers, lift_ref[2 * width :])
        + bias_ref[...]
    )


def by_live(count, slots, body):
    part = slots // 4
    for quarter in range(1, 5):
        low = (quarter - 1) * part if quarter > 1 else -1

        @pl.when((count > low) & (count <= quarter * part))
        def _(rows=quarter * part):
            body(rows)


def load_pieces(step, sources, held_ref, sems):
    copies, start = [], 0
    for place, source in enumerate(sources):
        size = source.shape[0]
        copies.append(
            (start, pltpu.make_async_copy(source, held_ref.at[pl.ds(start, size)], sems.at[place]))
        )
        start += size

    @pl.when(step == 0)
    def _():
        for _, copy in copies:
            copy.start()

    for first, copy in copies:

        @pl.when(step == first)
        def _(copy=copy):
            copy.wait()


def forward_kernel(pieces, first, last, *refs):
    refs = list(refs)
    take = lambda size: [refs.pop(0) for _ in range(size)]
    owner_ref, live_ref, order_ref, mine_ref = take(4)
    sources = take(pieces)
    pre_ref, receiver_ref, nodes_ref, lift_ref, mix_ref, gain_ref = take(6)
    if not first:
        take(4)
        (carried_ref,) = take(1)
    if last:
        seed_ref, node_lift_hbm, node_bias_ref, node_mix_hbm, node_gain_ref = take(5)
    hidden_ref, normed_ref, slope_ref, inverse_ref = take(4)
    if last:
        base_ref, summed_grad_ref, packed_ref, small_ref = take(4)
    else:
        (summed_ref,) = take(1)
    held_ref, sems = take(2)
    if last:
        summed_ref, total_ref, node_lift_ref, node_mix_ref, weight_sems = take(5)
    step = pl.program_id(0)
    count, width = nodes_ref.shape
    load_pieces(step, sources, held_ref, sems)
    if last:
        loads = [
            pltpu.make_async_copy(node_lift_hbm, node_lift_ref, weight_sems.at[0]),
            pltpu.make_async_copy(node_mix_hbm, node_mix_ref, weight_sems.at[1]),
        ]

    @pl.when(step == 0)
    def _():
        if last:
            for load in loads:
                load.start()
        summed_ref[...] = jnp.zeros_like(summed_ref) if first else carried_ref[...]

    owner = owner_ref[step]
    live_count = live_ref[owner]
    slots = pre_ref.shape[1]

    def body(rows):
        index = pick_row(held_ref[step, count:, :rows], mine_ref[0])
        senders = contract_rows(one_hot(index, count), held_ref[step, :count]).astype(BF16)
        pre = pre_ref[0, :rows] + matmul(senders, lift_ref[...])
        hidden, slope = silu_pair(pre)
        hidden = hidden.astype(BF16)
        normed, inverse = norm_forward(matmul(hidden, mix_ref[...]))
        hidden_ref[0, :rows] = hidden
        slope_ref[0, :rows] = slope.astype(BF16)
        normed_ref[0, :rows] = normed.astype(BF16)
        inverse_ref[0, :rows] = inverse
        if rows < slots:
            for saved_ref in (hidden_ref, slope_ref, normed_ref, inverse_ref):
                saved_ref[0, rows:] = jnp.zeros_like(saved_ref[0, rows:])
        live = live_rows(live_count, normed.shape)
        message = jnp.where(live, normed * gain_ref[...], 0.0).astype(BF16)
        summed_ref[...] += matmul(one_hot(receiver_ref[pl.ds(owner, 1), :][:, :rows], count), message)

    by_live(live_count, slots, body)

    if not last:
        return

    @pl.when(step == pl.num_programs(0) - 1)
    def _():
        for load in loads:
            load.wait()
        nodes = nodes_ref[...]
        summed = summed_ref[...].astype(BF16)
        pre_node = (
            matmul(nodes, node_lift_ref[:width])
            + matmul(summed, node_lift_ref[width:])
            + node_bias_ref[...]
        )
        hidden_node, slope_node = silu_pair(pre_node)
        hidden_node = hidden_node.astype(BF16)
        normed_node, inverse_node = norm_forward(matmul(hidden_node, node_mix_ref[...]))
        seed = seed_ref[...].astype(F32)
        small_ref[1:2, :] = jnp.sum(seed * normed_node, axis=0, keepdims=True)
        grad_out = norm_backward(seed * node_gain_ref[...], normed_node, inverse_node).astype(BF16)
        total_ref[2 * width :, :] = contract_rows(hidden_node, grad_out)
        grad_pre = (contract_features(grad_out, node_mix_ref[...]) * slope_node).astype(BF16)
        small_ref[0:1, :] = jnp.sum(grad_pre.astype(F32), axis=0, keepdims=True)
        total_ref[:width, :] = contract_rows(nodes, grad_pre)
        total_ref[width : 2 * width, :] = contract_rows(summed, grad_pre)
        base_ref[...] = seed + contract_features(grad_pre, node_lift_ref[:width])
        summed_grad_ref[...] = contract_features(grad_pre, node_lift_ref[width:]).astype(BF16)
        store_chunks(order_ref, total_ref, packed_ref, width)


def backward_kernel(pieces, *refs):
    arrival_ref, live_ref, order_ref, mine_ref = refs[:4]
    sources = refs[4 : 4 + pieces]
    (
        edges_ref,
        seed_ref,
        receiver_ref,
        hidden_ref,
        normed_ref,
        slope_ref,
        inverse_ref,
        nodes_ref,
        base_ref,
        summed_grad_ref,
        lift_ref,
        mix_ref,
        gain_ref,
        grad_edges_ref,
        partial_ref,
        grad_nodes_ref,
        packed_ref,
        small_ref,
        received_ref,
        total_ref,
        held_ref,
        out_ref,
        pre_ref,
        sent_ref,
        sems,
    ) = refs[4 + pieces :]
    step = pl.program_id(0)
    count, width = nodes_ref.shape
    group, slots = edges_ref.shape[:2]
    rows = group * slots
    copies, start = [], 0
    for place, source in enumerate(sources):
        size = source.shape[0]
        copies.append(
            pltpu.make_async_copy(source, held_ref.at[pl.ds(start, size)], sems.at[place])
        )
        start += size

    @pl.when(step == 0)
    def _():
        for copy in copies:
            copy.start()
        received_ref[...] = jnp.zeros_like(received_ref)
        total_ref[...] = jnp.zeros_like(total_ref)
        small_ref[...] = jnp.zeros_like(small_ref)

    tables = []
    for member in range(group):
        owner = step * group + member
        seed = seed_ref[member].astype(F32)
        live = live_rows(live_ref[owner], seed.shape)
        table = one_hot(receiver_ref[pl.ds(owner, 1), :], count)
        tables.append(table)
        grad_message = jnp.where(
            live, seed + contract_rows(table, summed_grad_ref[...]), 0.0
        )
        normed = normed_ref[member].astype(F32)
        small_ref[1:2, :] += jnp.sum(grad_message * normed, axis=0, keepdims=True)
        grad_out = norm_backward(
            grad_message * gain_ref[...], normed, inverse_ref[member]
        ).astype(BF16)
        grad_pre = (
            contract_features(grad_out, mix_ref[...]) * slope_ref[member].astype(F32)
        ).astype(BF16)
        out_ref[member * slots : (member + 1) * slots, :] = grad_out
        pre_ref[member * slots : (member + 1) * slots, :] = grad_pre
        small_ref[0:1, :] += jnp.sum(grad_pre.astype(F32), axis=0, keepdims=True)
        grad_edges_ref[member] = jnp.where(
            live, seed + contract_features(grad_pre, lift_ref[:width]), 0.0
        ).astype(BF16)

    @pl.when(step == 0)
    def _():
        for copy in copies:
            copy.wait()

    first_arrival = (arrival_ref[step * group] // group) * group
    for member in range(group):
        arrival = arrival_ref[step * group + member]
        place = arrival - first_arrival
        index = pick_row(held_ref[arrival, count:, :slots], mine_ref[0])
        sent = matmul(
            one_hot(index, count), pre_ref[member * slots : (member + 1) * slots, :]
        ).astype(BF16)
        partial_ref[place % 2, place // 2] = sent
        sent_ref[place] = sent
    received_ref[...] += matmul(jnp.concatenate(tables, axis=1), pre_ref[...])
    total_ref[3 * width :, :] += contract_rows(
        hidden_ref[...].reshape(rows, width), out_ref[...]
    )
    total_ref[:width, :] += contract_rows(edges_ref[...].reshape(rows, width), pre_ref[...])
    total_ref[width : 2 * width, :] += contract_rows(
        held_ref[pl.ds(first_arrival, group), :count].reshape(group * count, width),
        sent_ref[...].reshape(group * count, width),
    )

    @pl.when(step == pl.num_programs(0) - 1)
    def _():
        received = received_ref[...].astype(BF16)
        total_ref[2 * width : 3 * width, :] = contract_rows(nodes_ref[...], received)
        grad_nodes_ref[...] = base_ref[...] + contract_features(received, lift_ref[2 * width :])
        store_chunks(order_ref, total_ref, packed_ref, width)


def unpack_kernel(scale, places, *refs):
    order_ref = refs[0]
    sources = refs[1 : 1 + len(places)]
    targets = refs[-9:-5]
    buffers = refs[-5:-1]
    sems = refs[-1]
    parts = [target.shape[0] // CHUNKS for target in targets]
    copies, slot = [], 0
    for source, place in zip(sources, places):
        for start in range(0, source.shape[0], sum(parts)):
            for kind, rows in enumerate(parts):
                held = buffers[kind].at[pl.ds(slot * rows, rows)]
                held[...] = source[start : start + rows, :].astype(F32) * scale[kind // 2]
                target = pl.multiple_of(order_ref[place] * rows, 16)
                copies.append(
                    pltpu.make_async_copy(
                        held, targets[kind].at[pl.ds(target, rows)], sems.at[kind, slot]
                    )
                )
                copies[-1].start()
                start += rows
            slot += 1
            place += 1
    for copy in copies:
        copy.wait()


def swap(values, axis, bit):
    size = lax.axis_size(axis)
    return lax.ppermute(values, axis, [(i, i ^ bit) for i in range(size)])


def add_rounded(left, right):
    return (left.astype(F32) + right.astype(F32)).astype(BF16)


def exchange(*moves):
    values = lax.optimization_barrier(tuple(move[0] for move in moves))
    moved = [swap(value, axis, bit) for value, (_, axis, bit) in zip(values, moves)]
    return lax.optimization_barrier(tuple(moved))


def halves(part):
    rows = part.shape[0] // 2
    return part[:rows], part[rows:]


def halves_inner(blocks):
    rows = blocks.shape[1] // 2
    return blocks[:, :rows], blocks[:, rows:]


def join(*parts):
    return jnp.concatenate(parts)


def node_start(node_packed):
    sides = [halves(side) for side in halves(node_packed)]
    got = [swap(sides[0][1], "grp", 1), swap(sides[1][1], "grp", 2)]
    return [side[0] for side in sides], got


def reduce_all(edge_packed, node_kept, node_got, partial, small):
    node_a, node_b = [add_rounded(kept, got) for kept, got in zip(node_kept, node_got)]

    keep, send = halves(edge_packed)
    got, got_small, got_partial = exchange(
        (send, "dev", 1), (small, "dev", 1), (partial[1], "dev", 1)
    )
    edge_a, edge_b = halves(add_rounded(keep, got))
    small = small + got_small
    owned = add_rounded(partial[0], got_partial)
    owned_early, owned_late = halves_inner(owned)

    keep_a, send_a = halves(edge_a)
    keep_b, send_b = halves(edge_b)
    node_keep_a, node_send_a = halves(node_a)
    node_keep_b, node_send_b = halves(node_b)
    got_a, got_b, got_node, got_small, got_owned = exchange(
        (send_a, "grp", 1),
        (send_b, "grp", 2),
        (join(node_send_a, node_send_b), "dev", 1),
        (small, "grp", 1),
        (owned_early[1::2], "dev", 2),
    )
    edge_a, edge_b = add_rounded(keep_a, got_a), add_rounded(keep_b, got_b)
    got_node_a, got_node_b = halves(got_node)
    node_a, node_b = add_rounded(node_keep_a, got_node_a), add_rounded(node_keep_b, got_node_b)
    small = small + got_small
    owned_early = add_rounded(owned_early[::2], got_owned)

    pairs = [halves(part) for part in (edge_a, node_a, edge_b, node_b)]
    got_a, got_b, got_small, got_owned, got_early = exchange(
        (join(pairs[0][1], pairs[1][1]), "grp", 2),
        (join(pairs[2][1], pairs[3][1]), "grp", 1),
        (small, "grp", 2),
        (owned_late[1::2], "dev", 2),
        (owned_early[1], "dev", 4),
    )
    small = small + got_small
    owned_late = add_rounded(owned_late[::2], got_owned)
    edge_rows = pairs[0][0].shape[0]
    parts = [
        halves(add_rounded(pairs[0][0], got_a[:edge_rows])),
        halves(add_rounded(pairs[1][0], got_a[edge_rows:])),
        halves(add_rounded(pairs[2][0], got_b[:edge_rows])),
        halves(add_rounded(pairs[3][0], got_b[edge_rows:])),
    ]
    got_1, got_2, got_3, got_small = exchange(
        (join(parts[0][1], parts[1][1]), "dev", 2),
        (join(parts[2][0], parts[3][0]), "dev", 4),
        (join(parts[2][1], parts[3][1]), "dev", 6),
        (small, "dev", 2),
    )
    small = small + got_small
    kept = sum(
        (got.astype(F32) for got in (got_1, got_2, got_3)),
        join(parts[0][0], parts[1][0]).astype(F32),
    ).astype(BF16)
    got_1, got_2, got_3, got_small = exchange(
        (kept, "dev", 2), (kept, "dev", 4), (kept, "dev", 6), (small, "dev", 4)
    )
    small = small + got_small

    side_a, side_b = join(kept, got_1), join(got_2, got_3)
    got_a, got_b, got_late = exchange(
        (side_a, "grp", 2), (side_b, "grp", 1), (owned_late[1], "dev", 4)
    )
    from_senders = join(owned_early[0], owned_late[0]).astype(F32) + join(
        got_early, got_late
    ).astype(F32)
    side_a, side_b = join(side_a, got_a), join(side_b, got_b)
    got_a, got_b, swapped_a, swapped_b = exchange(
        (side_a, "grp", 1),
        (side_b, "grp", 2),
        (side_a, "dev", 1),
        (side_b, "dev", 1),
    )
    last_a, last_b = exchange((got_a, "dev", 1), (got_b, "dev", 1))
    sources = [
        [(side_a, 0), (side_b, 8)],
        [
            (got_a, 4),
            (got_b, 12),
            (swapped_a, 16),
            (swapped_b, 24),
            (last_a, 20),
            (last_b, 28),
        ],
    ]
    return sources, small, from_senders


def device_bits():
    group = lax.axis_index("grp")
    device = lax.axis_index("dev")
    return group & 1, group >> 1, device & 1, (device >> 1) & 1, (device >> 2) & 1


def relative_places(place):
    x, y, core, z, far = device_bits()
    mirrored = (place & 25) | ((place & 4) >> 1) | ((place & 2) << 1)
    plain = jnp.where((place & 8) == 0, place, mirrored)
    return plain ^ (core * 16 + far * 8 + x * 4 + y * 2 + z)


def edge_order():
    return relative_places(jnp.arange(CHUNKS, dtype=jnp.int32))


def node_order():
    place = jnp.arange(CHUNKS, dtype=jnp.int32)
    return relative_places(((place & 4) << 2) | ((place & 24) >> 1) | (place & 3))


def shape(*dims, kind=F32):
    return jax.ShapeDtypeStruct(dims, kind)


def params(mebibytes):
    return pltpu.CompilerParams(vmem_limit_bytes=mebibytes << 20)


def whole(*dims):
    return pl.BlockSpec(dims, lambda *_: (0,) * len(dims), pipeline_mode=pl.Buffered(1))


def result(*dims):
    return pl.BlockSpec(dims, lambda *_: (0,) * len(dims))


def per_device(
    node_latent,
    edge_latent,
    node_cotangent,
    edge_cotangent,
    edge_sender,
    edge_receiver,
    live_counts,
    edge_lift,
    edge_bias,
    edge_mix,
    edge_gain,
    node_lift,
    node_bias,
    node_mix,
    node_gain,
):
    width = node_latent.shape[2]
    nodes = node_latent[0]
    count = nodes.shape[0]
    peers = edge_receiver.shape[1]
    slots = edge_receiver.shape[2]
    total_rows = peers * slots
    unit = total_rows * width * width
    edges = edge_latent.reshape(peers, slots, width)
    edge_seed = edge_cotangent.reshape(peers, slots, width)
    receivers = edge_receiver.reshape(peers, slots)
    live = live_counts.reshape(peers)
    mine = lax.axis_index("dev")
    paired = lax.axis_size("dev") == 8 and lax.axis_size("grp") == 4
    packed_rows = count + -(-peers // 16) * 16
    packed_nodes = pl.pallas_call(
        pack_kernel,
        out_shape=shape(packed_rows, width, kind=BF16),
        compiler_params=params(4),
        name="pack",
    )(nodes, edge_sender)
    if paired:
        owners = jnp.arange(peers, dtype=jnp.int32) ^ mine
        edge_places = edge_order()
        node_places = node_order()
        near = swap(packed_nodes, "dev", 2)
        across = swap(packed_nodes, "dev", 4)
        beside, across = lax.optimization_barrier((swap(packed_nodes, "dev", 1), across))
        behind = swap(across, "dev", 2)
        pieces = [packed_nodes, beside]
        pieces = [piece[None] for piece in pieces]
        ranges = [(0, 2), (2, 6), (6, 8)]
    else:
        owners = jnp.arange(peers, dtype=jnp.int32)
        edge_places = node_places = jnp.arange(CHUNKS, dtype=jnp.int32)
        pieces = [lax.all_gather(packed_nodes, "dev")]
        ranges = [(0, peers)]
    gathered_rows = pieces[0].shape[1]

    anywhere = pl.BlockSpec(memory_space=pl.ANY)
    bias_row = edge_bias.reshape(1, width)
    gain_row = edge_gain.reshape(1, width)

    owned = pl.BlockSpec((1, slots, width), lambda i: (i, 0, 0))
    pre = pl.pallas_call(
        lift_kernel,
        grid=(peers,),
        in_specs=[
            owned,
            whole(peers, slots),
            whole(count, width),
            whole(3 * width, width),
            whole(1, width),
        ],
        out_specs=owned,
        out_shape=shape(peers, slots, width),
        compiler_params=params(12),
        cost_estimate=pl.CostEstimate(
            flops=5 * unit, bytes_accessed=6 * total_rows * width, transcendentals=0
        ),
        name="lift",
    )(edges, receivers, nodes, edge_lift, bias_row)

    def by_owner(*dims):
        return pl.BlockSpec(
            (1,) + dims, lambda i, owner, *_: (owner[i],) + (0,) * len(dims)
        )

    group = 2

    def grouped(*dims):
        return pl.BlockSpec((group,) + dims, lambda i, *_: (i,) + (0,) * len(dims))

    saved = []
    summed = None
    for begin, end in ranges:
        first, last = begin == 0, end == peers
        if last and not first:
            behind, summed = lax.optimization_barrier((behind, summed))
        if not first:
            for piece in [behind] if last else [near, across]:
                pieces += [piece[None], swap(piece, "dev", 1)[None]]
        chosen = pieces[begin:] if paired else pieces

        operands = chosen + [
            pre,
            receivers,
            nodes,
            edge_lift,
            edge_mix,
            gain_row,
        ]
        in_specs = [anywhere] * len(chosen) + [
            by_owner(slots, width),
            whole(peers, slots),
            whole(count, width),
            pl.BlockSpec((width, width), lambda *_: (1, 0), pipeline_mode=pl.Buffered(1)),
            whole(width, width),
            whole(1, width),
        ]
        aliases = {}
        if not first:
            aliases = {4 + len(operands) + j: j for j in range(4)}
            operands += saved + [summed]
            in_specs += [anywhere] * 4 + [whole(count, width)]
        out_specs = [by_owner(slots, width)] * 3 + [by_owner(slots, 1)]
        out_shape = [shape(peers, slots, width, kind=BF16)] * 3 + [shape(peers, slots, 1)]
        scratch = [
            pltpu.VMEM((end - begin, gathered_rows, width), BF16),
            pltpu.SemaphoreType.DMA((len(chosen),)),
        ]
        if last:
            operands += [
                node_cotangent[0],
                node_lift,
                node_bias.reshape(1, width),
                node_mix,
                node_gain.reshape(1, width),
            ]
            in_specs += [whole(count, width), anywhere, whole(1, width), anywhere, whole(1, width)]
            out_specs += [
                result(count, width),
                result(count, width),
                result(3 * width, width),
                result(2, width),
            ]
            out_shape += [
                shape(count, width),
                shape(count, width, kind=BF16),
                shape(3 * width, width, kind=BF16),
                shape(2, width),
            ]
            scratch += [
                pltpu.VMEM((count, width), F32),
                pltpu.VMEM((3 * width, width), F32),
                pltpu.VMEM((2 * width, width), BF16),
                pltpu.VMEM((width, width), BF16),
                pltpu.SemaphoreType.DMA((2,)),
            ]
        else:
            out_specs.append(result(count, width))
            out_shape.append(shape(count, width))
        results = pl.pallas_call(
            functools.partial(forward_kernel, len(chosen), first, last),
            grid_spec=pltpu.PrefetchScalarGridSpec(
                num_scalar_prefetch=4,
                grid=(end - begin,),
                in_specs=in_specs,
                out_specs=out_specs,
                scratch_shapes=scratch,
            ),
            out_shape=out_shape,
            input_output_aliases=aliases,
            compiler_params=params(24),
            cost_estimate=pl.CostEstimate(
                flops=4 * unit,
                bytes_accessed=8 * total_rows * width,
                transcendentals=total_rows * width,
            ),
            name="forward_%d" % begin,
        )(owners[begin:end], live, node_places, mine.reshape(1), *operands)
        saved = list(results[:4])
        if last:
            base, summed_grad, node_packed, node_small = results[4:]
        else:
            summed = results[4]
    hidden, normed, slope, inverse = saved

    if paired:
        node_kept, node_got = node_start(node_packed)
    grad_edges, partial, grad_nodes, edge_packed, edge_small = pl.pallas_call(
        functools.partial(backward_kernel, len(pieces)),
        grid_spec=pltpu.PrefetchScalarGridSpec(
            num_scalar_prefetch=4,
            grid=(peers // group,),
            in_specs=[anywhere] * len(pieces)
            + [
                grouped(slots, width),
                grouped(slots, width),
                whole(peers, slots),
                grouped(slots, width),
                grouped(slots, width),
                grouped(slots, width),
                grouped(slots, 1),
                whole(count, width),
                whole(count, width),
                whole(count, width),
                whole(3 * width, width),
                whole(width, width),
                whole(1, width),
            ],
            out_specs=[
                grouped(slots, width),
                pl.BlockSpec(
                    (2, group // 2, count, width),
                    lambda i, arrival, *_: (0, arrival[i * group] // group, 0, 0),
                ),
                result(count, width),
                result(4 * width, width),
                result(2, width),
            ],
            scratch_shapes=[
                pltpu.VMEM((count, width), F32),
                pltpu.VMEM((4 * width, width), F32),
                pltpu.VMEM((peers, gathered_rows, width), BF16),
                pltpu.VMEM((group * slots, width), BF16),
                pltpu.VMEM((group * slots, width), BF16),
                pltpu.VMEM((group, count, width), BF16),
                pltpu.SemaphoreType.DMA((len(pieces),)),
            ],
        ),
        out_shape=[
            shape(peers, slots, width, kind=BF16),
            shape(2, peers // 2, count, width, kind=BF16),
            shape(count, width),
            shape(4 * width, width, kind=BF16),
            shape(2, width),
        ],
        compiler_params=params(30),
        cost_estimate=pl.CostEstimate(
            flops=14 * unit, bytes_accessed=20 * total_rows * width, transcendentals=0
        ),
        name="backward",
    )(
        owners,
        live,
        edge_places,
        mine.reshape(1),
        *pieces,
        edges,
        edge_seed,
        receivers,
        hidden,
        normed,
        slope,
        inverse,
        nodes,
        base,
        summed_grad,
        edge_lift,
        edge_mix,
        gain_row,
    )

    if paired:
        edge_packed, edge_small, *node_got = lax.optimization_barrier(
            (edge_packed, edge_small, *node_got)
        )
    small = jnp.concatenate([edge_small, node_small])
    if paired:
        sources, small, from_senders = reduce_all(
            edge_packed, node_kept, node_got, partial, small
        )
    else:
        node_sum, edge_sum, small = lax.psum(
            (node_packed.astype(F32), edge_packed.astype(F32), small), ("grp", "dev")
        )
        interleaved = jnp.concatenate(
            [
                edge_sum.reshape(CHUNKS, 4 * width // CHUNKS, width),
                node_sum.reshape(CHUNKS, 3 * width // CHUNKS, width),
            ],
            axis=1,
        )
        sources = [[(interleaved.reshape(7 * width, width).astype(BF16), 0)]]
        ordered = jnp.swapaxes(partial, 0, 1).reshape(peers, count, width)
        from_senders = lax.psum_scatter(ordered.astype(F32), "dev", scatter_dimension=0)
    grad_nodes = grad_nodes + contract_features(
        from_senders.astype(BF16), edge_lift[width : 2 * width]
    )
    groups = lax.axis_size("grp") * lax.axis_size("dev")
    edge_scale = float(total_rows * groups) ** (-0.5)
    node_scale = float(count * groups) ** (-0.5)
    totals = [3 * width, width, 2 * width, width]
    unpacked = []
    for part in sources:
        part, starts = zip(*part)
        places = sum(source.shape[0] for source in part) * CHUNKS // (7 * width)
        unpacked = pl.pallas_call(
            functools.partial(unpack_kernel, (edge_scale, node_scale), starts),
            grid_spec=pltpu.PrefetchScalarGridSpec(
                num_scalar_prefetch=1,
                grid=(1,),
                in_specs=[whole(*source.shape) for source in part] + [anywhere] * len(unpacked),
                out_specs=[anywhere] * 4,
                scratch_shapes=[
                    pltpu.VMEM((places * total // CHUNKS, width), F32) for total in totals
                ]
                + [pltpu.SemaphoreType.DMA((4, places))],
            ),
            out_shape=[shape(total, width) for total in totals],
            input_output_aliases={1 + len(part) + j: j for j in range(len(unpacked))},
            compiler_params=params(20),
            cost_estimate=pl.CostEstimate(
                flops=0, bytes_accessed=42 * places * width * width // CHUNKS, transcendentals=0
            ),
            name="unpack_%d" % starts[0],
        )(edge_places, *part, *unpacked)
    edge_lift_grad, edge_mix_grad, node_lift_grad, node_mix_grad = unpacked
    return (
        grad_nodes[None],
        grad_edges.reshape(1, 1, peers, slots, width),
        edge_lift_grad,
        small[0] * edge_scale,
        edge_mix_grad,
        small[1] * edge_scale,
        node_lift_grad,
        small[2] * node_scale,
        node_mix_grad,
        small[3] * node_scale,
    )


def solution(mesh):
    return jax.shard_map(
        per_device,
        mesh=mesh,
        in_specs=(
            P("grp", "dev", None),
            P("grp", "dev", None, None, None),
            P("grp", "dev", None),
            P("grp", "dev", None, None, None),
            P(None, "dev", None),
            P("dev", None, None),
            P("dev", None),
            P(),
            P(),
            P(),
            P(),
            P(),
            P(),
            P(),
            P(),
        ),
        out_specs=(
            P("grp", "dev", None),
            P("grp", "dev", None, None, None),
            P(),
            P(),
            P(),
            P(),
            P(),
            P(),
            P(),
            P(),
        ),
        check_vma=False,
    )
```

```python
import functools

import jax
import jax.numpy as jnp
from jax import lax
from jax.experimental import pallas as pl
from jax.experimental.pallas import tpu as pltpu
from jax.sharding import PartitionSpec as P

EPSILON = 1e-05
CHUNKS = 32
BF16 = jnp.bfloat16
F32 = jnp.float32


def matmul(left, right):
    return jnp.dot(left, right, preferred_element_type=F32)


def contract_rows(left, right):
    return lax.dot_general(left, right, (((0,), (0,)), ((), ())), preferred_element_type=F32)


def contract_features(left, right):
    return lax.dot_general(left, right, (((1,), (1,)), ((), ())), preferred_element_type=F32)


def one_hot(index_row, nodes):
    rows = lax.broadcasted_iota(jnp.int32, (nodes, index_row.shape[1]), 0)
    return jnp.where(rows == index_row, 1.0, 0.0).astype(BF16)


def silu_pair(values):
    gate = 0.5 * jnp.tanh(0.5 * values) + 0.5
    hidden = values * gate
    return hidden, gate + hidden * (1.0 - gate)


def norm_forward(values):
    centred = values - jnp.mean(values, axis=-1, keepdims=True)
    inverse = lax.rsqrt(jnp.mean(centred * centred, axis=-1, keepdims=True) + EPSILON)
    return centred * inverse, inverse


def norm_backward(grad_hat, normed, inverse):
    spread = jnp.mean(grad_hat * normed, axis=-1, keepdims=True)
    return inverse * (grad_hat - jnp.mean(grad_hat, axis=-1, keepdims=True) - normed * spread)


def pick_row(block, place):
    rows = lax.broadcasted_iota(jnp.int32, block.shape, 0)
    picked = jnp.sum(jnp.where(rows == place, block.astype(F32), 0.0), axis=0, keepdims=True)
    return picked.astype(jnp.int32)


def pack_kernel(nodes_ref, sender_ref, packed_ref):
    count, width = nodes_ref.shape
    peers, _, slots = sender_ref.shape
    packed_ref[:count] = nodes_ref[...]
    packed_ref[count:] = jnp.zeros((packed_ref.shape[0] - count, width), BF16)
    packed_ref[count : count + peers, :slots] = sender_ref[:, 0, :].astype(F32).astype(BF16)


def live_rows(count, shape):
    return lax.broadcasted_iota(jnp.int32, shape, 0) < count


def store_chunks(order_ref, source_ref, target_ref, mix_rows):
    mix_part = mix_rows // CHUNKS
    rows = source_ref.shape[0] // CHUNKS
    lift_part = rows - mix_part
    lift_rows = lift_part * CHUNKS

    def step(place, carry):
        chunk = order_ref[place]
        target = pl.multiple_of(place * rows, 16)
        lift_start = pl.multiple_of(chunk * lift_part, 16)
        mix_start = pl.multiple_of(lift_rows + chunk * mix_part, 16)
        target_ref[pl.ds(target, lift_part), :] = source_ref[
            pl.ds(lift_start, lift_part), :
        ].astype(BF16)
        target_ref[pl.ds(pl.multiple_of(target + lift_part, 16), mix_part), :] = source_ref[
            pl.ds(mix_start, mix_part), :
        ].astype(BF16)
        return carry

    lax.fori_loop(0, CHUNKS, step, 0)


def lift_kernel(edges_ref, receiver_ref, nodes_ref, lift_ref, bias_ref, pre_ref):
    width = nodes_ref.shape[1]
    table = one_hot(receiver_ref[pl.ds(pl.program_id(0), 1), :], nodes_ref.shape[0])
    receivers = contract_rows(table, nodes_ref[...]).astype(BF16)
    pre_ref[0] = (
        matmul(edges_ref[0], lift_ref[:width])
        + matmul(receivers, lift_ref[2 * width :])
        + bias_ref[...]
    )


def by_live(count, slots, body):
    part = slots // 4
    for quarter in range(1, 5):
        low = (quarter - 1) * part if quarter > 1 else -1

        @pl.when((count > low) & (count <= quarter * part))
        def _(rows=quarter * part):
            body(rows)


def load_pieces(step, sources, held_ref, sems):
    copies, start = [], 0
    for place, source in enumerate(sources):
        size = source.shape[0]
        copies.append(
            (start, pltpu.make_async_copy(source, held_ref.at[pl.ds(start, size)], sems.at[place]))
        )
        start += size

    @pl.when(step == 0)
    def _():
        for _, copy in copies:
            copy.start()

    for first, copy in copies:

        @pl.when(step == first)
        def _(copy=copy):
            copy.wait()


def forward_kernel(pieces, first, last, *refs):
    refs = list(refs)
    take = lambda size: [refs.pop(0) for _ in range(size)]
    owner_ref, live_ref, order_ref, mine_ref = take(4)
    sources = take(pieces)
    pre_ref, receiver_ref, nodes_ref, lift_ref, mix_ref, gain_ref = take(6)
    if not first:
        take(4)
        (carried_ref,) = take(1)
    if last:
        seed_ref, node_lift_hbm, node_bias_ref, node_mix_hbm, node_gain_ref = take(5)
    hidden_ref, normed_ref, slope_ref, inverse_ref = take(4)
    if last:
        base_ref, summed_grad_ref, packed_ref, small_ref = take(4)
    else:
        (summed_ref,) = take(1)
    held_ref, sems = take(2)
    if last:
        summed_ref, total_ref, node_lift_ref, node_mix_ref, weight_sems = take(5)
    step = pl.program_id(0)
    count, width = nodes_ref.shape
    load_pieces(step, sources, held_ref, sems)
    if last:
        loads = [
            pltpu.make_async_copy(node_lift_hbm, node_lift_ref, weight_sems.at[0]),
            pltpu.make_async_copy(node_mix_hbm, node_mix_ref, weight_sems.at[1]),
        ]

    @pl.when(step == 0)
    def _():
        if last:
            for load in loads:
                load.start()
        summed_ref[...] = jnp.zeros_like(summed_ref) if first else carried_ref[...]

    owner = owner_ref[step]
    live_count = live_ref[owner]
    slots = pre_ref.shape[1]

    def body(rows):
        index = pick_row(held_ref[step, count:, :rows], mine_ref[0])
        senders = contract_rows(one_hot(index, count), held_ref[step, :count]).astype(BF16)
        pre = pre_ref[0, :rows] + matmul(senders, lift_ref[...])
        hidden, slope = silu_pair(pre)
        hidden = hidden.astype(BF16)
        normed, inverse = norm_forward(matmul(hidden, mix_ref[...]))
        hidden_ref[0, :rows] = hidden
        slope_ref[0, :rows] = slope.astype(BF16)
        normed_ref[0, :rows] = normed.astype(BF16)
        inverse_ref[0, :rows] = inverse
        if rows < slots:
            for saved_ref in (hidden_ref, slope_ref, normed_ref, inverse_ref):
                saved_ref[0, rows:] = jnp.zeros_like(saved_ref[0, rows:])
        live = live_rows(live_count, normed.shape)
        message = jnp.where(live, normed * gain_ref[...], 0.0).astype(BF16)
        summed_ref[...] += matmul(one_hot(receiver_ref[pl.ds(owner, 1), :][:, :rows], count), message)

    by_live(live_count, slots, body)

    if not last:
        return

    @pl.when(step == pl.num_programs(0) - 1)
    def _():
        for load in loads:
            load.wait()
        nodes = nodes_ref[...]
        summed = summed_ref[...].astype(BF16)
        pre_node = (
            matmul(nodes, node_lift_ref[:width])
            + matmul(summed, node_lift_ref[width:])
            + node_bias_ref[...]
        )
        hidden_node, slope_node = silu_pair(pre_node)
        hidden_node = hidden_node.astype(BF16)
        normed_node, inverse_node = norm_forward(matmul(hidden_node, node_mix_ref[...]))
        seed = seed_ref[...].astype(F32)
        small_ref[1:2, :] = jnp.sum(seed * normed_node, axis=0, keepdims=True)
        grad_out = norm_backward(seed * node_gain_ref[...], normed_node, inverse_node).astype(BF16)
        total_ref[2 * width :, :] = contract_rows(hidden_node, grad_out)
        grad_pre = (contract_features(grad_out, node_mix_ref[...]) * slope_node).astype(BF16)
        small_ref[0:1, :] = jnp.sum(grad_pre.astype(F32), axis=0, keepdims=True)
        total_ref[:width, :] = contract_rows(nodes, grad_pre)
        total_ref[width : 2 * width, :] = contract_rows(summed, grad_pre)
        base_ref[...] = seed + contract_features(grad_pre, node_lift_ref[:width])
        summed_grad_ref[...] = contract_features(grad_pre, node_lift_ref[width:]).astype(BF16)
        store_chunks(order_ref, total_ref, packed_ref, width)


def backward_kernel(pieces, *refs):
    arrival_ref, live_ref, order_ref, mine_ref = refs[:4]
    sources = refs[4 : 4 + pieces]
    (
        edges_ref,
        seed_ref,
        receiver_ref,
        hidden_ref,
        normed_ref,
        slope_ref,
        inverse_ref,
        nodes_ref,
        base_ref,
        summed_grad_ref,
        lift_ref,
        mix_ref,
        gain_ref,
        grad_edges_ref,
        partial_ref,
        grad_nodes_ref,
        packed_ref,
        small_ref,
        received_ref,
        total_ref,
        held_ref,
        out_ref,
        pre_ref,
        sent_ref,
        sems,
    ) = refs[4 + pieces :]
    step = pl.program_id(0)
    count, width = nodes_ref.shape
    group, slots = edges_ref.shape[:2]
    rows = group * slots
    copies, start = [], 0
    for place, source in enumerate(sources):
        size = source.shape[0]
        copies.append(
            pltpu.make_async_copy(source, held_ref.at[pl.ds(start, size)], sems.at[place])
        )
        start += size

    @pl.when(step == 0)
    def _():
        for copy in copies:
            copy.start()
        received_ref[...] = jnp.zeros_like(received_ref)
        total_ref[...] = jnp.zeros_like(total_ref)
        small_ref[...] = jnp.zeros_like(small_ref)

    tables = []
    for member in range(group):
        owner = step * group + member
        seed = seed_ref[member].astype(F32)
        live = live_rows(live_ref[owner], seed.shape)
        table = one_hot(receiver_ref[pl.ds(owner, 1), :], count)
        tables.append(table)
        grad_message = jnp.where(
            live, seed + contract_rows(table, summed_grad_ref[...]), 0.0
        )
        normed = normed_ref[member].astype(F32)
        small_ref[1:2, :] += jnp.sum(grad_message * normed, axis=0, keepdims=True)
        grad_out = norm_backward(
            grad_message * gain_ref[...], normed, inverse_ref[member]
        ).astype(BF16)
        grad_pre = (
            contract_features(grad_out, mix_ref[...]) * slope_ref[member].astype(F32)
        ).astype(BF16)
        out_ref[member * slots : (member + 1) * slots, :] = grad_out
        pre_ref[member * slots : (member + 1) * slots, :] = grad_pre
        small_ref[0:1, :] += jnp.sum(grad_pre.astype(F32), axis=0, keepdims=True)
        grad_edges_ref[member] = jnp.where(
            live, seed + contract_features(grad_pre, lift_ref[:width]), 0.0
        ).astype(BF16)

    @pl.when(step == 0)
    def _():
        for copy in copies:
            copy.wait()

    first_arrival = (arrival_ref[step * group] // group) * group
    for member in range(group):
        arrival = arrival_ref[step * group + member]
        place = arrival - first_arrival
        index = pick_row(held_ref[arrival, count:, :slots], mine_ref[0])
        sent = matmul(
            one_hot(index, count), pre_ref[member * slots : (member + 1) * slots, :]
        ).astype(BF16)
        partial_ref[place % 2, place // 2] = sent
        sent_ref[place] = sent
    received_ref[...] += matmul(jnp.concatenate(tables, axis=1), pre_ref[...])
    total_ref[3 * width :, :] += contract_rows(
        hidden_ref[...].reshape(rows, width), out_ref[...]
    )
    total_ref[:width, :] += contract_rows(edges_ref[...].reshape(rows, width), pre_ref[...])
    total_ref[width : 2 * width, :] += contract_rows(
        held_ref[pl.ds(first_arrival, group), :count].reshape(group * count, width),
        sent_ref[...].reshape(group * count, width),
    )

    @pl.when(step == pl.num_programs(0) - 1)
    def _():
        received = received_ref[...].astype(BF16)
        total_ref[2 * width : 3 * width, :] = contract_rows(nodes_ref[...], received)
        grad_nodes_ref[...] = base_ref[...] + contract_features(received, lift_ref[2 * width :])
        store_chunks(order_ref, total_ref, packed_ref, width)


def unpack_kernel(scale, places, *refs):
    order_ref = refs[0]
    sources = refs[1 : 1 + len(places)]
    targets = refs[-9:-5]
    buffers = refs[-5:-1]
    sems = refs[-1]
    parts = [target.shape[0] // CHUNKS for target in targets]
    copies, slot = [], 0
    for source, place in zip(sources, places):
        for start in range(0, source.shape[0], sum(parts)):
            for kind, rows in enumerate(parts):
                held = buffers[kind].at[pl.ds(slot * rows, rows)]
                held[...] = source[start : start + rows, :].astype(F32) * scale[kind // 2]
                target = pl.multiple_of(order_ref[place] * rows, 16)
                copies.append(
                    pltpu.make_async_copy(
                        held, targets[kind].at[pl.ds(target, rows)], sems.at[kind, slot]
                    )
                )
                copies[-1].start()
                start += rows
            slot += 1
            place += 1
    for copy in copies:
        copy.wait()


def swap(values, axis, bit):
    size = lax.axis_size(axis)
    return lax.ppermute(values, axis, [(i, i ^ bit) for i in range(size)])


def add_rounded(left, right):
    return (left.astype(F32) + right.astype(F32)).astype(BF16)


def exchange(*moves):
    values = lax.optimization_barrier(tuple(move[0] for move in moves))
    moved = [swap(value, axis, bit) for value, (_, axis, bit) in zip(values, moves)]
    return lax.optimization_barrier(tuple(moved))


def halves(part):
    rows = part.shape[0] // 2
    return part[:rows], part[rows:]


def halves_inner(blocks):
    rows = blocks.shape[1] // 2
    return blocks[:, :rows], blocks[:, rows:]


def join(*parts):
    return jnp.concatenate(parts)


def node_start(node_packed):
    sides = [halves(side) for side in halves(node_packed)]
    got = [swap(sides[0][1], "grp", 1), swap(sides[1][1], "grp", 2)]
    return [side[0] for side in sides], got


def reduce_all(edge_packed, node_kept, node_got, partial, small):
    node_a, node_b = [add_rounded(kept, got) for kept, got in zip(node_kept, node_got)]

    keep, send = halves(edge_packed)
    got, got_small, got_partial = exchange(
        (send, "dev", 1), (small, "dev", 1), (partial[1], "dev", 1)
    )
    edge_a, edge_b = halves(add_rounded(keep, got))
    small = small + got_small
    owned = add_rounded(partial[0], got_partial)
    owned_early, owned_late = halves_inner(owned)

    keep_a, send_a = halves(edge_a)
    keep_b, send_b = halves(edge_b)
    node_keep_a, node_send_a = halves(node_a)
    node_keep_b, node_send_b = halves(node_b)
    got_a, got_b, got_node, got_small, got_owned = exchange(
        (send_a, "grp", 1),
        (send_b, "grp", 2),
        (join(node_send_a, node_send_b), "dev", 1),
        (small, "grp", 1),
        (owned_early[1::2], "dev", 2),
    )
    edge_a, edge_b = add_rounded(keep_a, got_a), add_rounded(keep_b, got_b)
    got_node_a, got_node_b = halves(got_node)
    node_a, node_b = add_rounded(node_keep_a, got_node_a), add_rounded(node_keep_b, got_node_b)
    small = small + got_small
    owned_early = add_rounded(owned_early[::2], got_owned)

    pairs = [halves(part) for part in (edge_a, node_a, edge_b, node_b)]
    got_a, got_b, got_small, got_owned, got_early = exchange(
        (join(pairs[0][1], pairs[1][1]), "grp", 2),
        (join(pairs[2][1], pairs[3][1]), "grp", 1),
        (small, "grp", 2),
        (owned_late[1::2], "dev", 2),
        (owned_early[1], "dev", 4),
    )
    small = small + got_small
    owned_late = add_rounded(owned_late[::2], got_owned)
    edge_rows = pairs[0][0].shape[0]
    parts = [
        halves(add_rounded(pairs[0][0], got_a[:edge_rows])),
        halves(add_rounded(pairs[1][0], got_a[edge_rows:])),
        halves(add_rounded(pairs[2][0], got_b[:edge_rows])),
        halves(add_rounded(pairs[3][0], got_b[edge_rows:])),
    ]
    got_1, got_2, got_3, got_small = exchange(
        (join(parts[0][1], parts[1][1]), "dev", 2),
        (join(parts[2][0], parts[3][0]), "dev", 4),
        (join(parts[2][1], parts[3][1]), "dev", 6),
        (small, "dev", 2),
    )
    small = small + got_small
    kept = sum(
        (got.astype(F32) for got in (got_1, got_2, got_3)),
        join(parts[0][0], parts[1][0]).astype(F32),
    ).astype(BF16)
    got_1, got_2, got_small = exchange((kept, "dev", 2), (kept, "dev", 4), (small, "dev", 4))
    got_3, got_late = exchange((got_2, "dev", 2), (owned_late[1], "dev", 4))
    small = small + got_small

    side_a, side_b = join(kept, got_1), join(got_2, got_3)
    got_a, got_b = exchange((side_a, "grp", 2), (side_b, "grp", 1))
    from_senders = join(owned_early[0], owned_late[0]).astype(F32) + join(
        got_early, got_late
    ).astype(F32)
    side_a, side_b = join(side_a, got_a), join(side_b, got_b)
    got_a, got_b, swapped_a, swapped_b = exchange(
        (side_a, "grp", 1),
        (side_b, "grp", 2),
        (side_a, "dev", 1),
        (side_b, "dev", 1),
    )
    last_a, last_b = exchange((got_a, "dev", 1), (got_b, "dev", 1))
    sources = [
        [(side_a, 0), (side_b, 8)],
        [
            (got_a, 4),
            (got_b, 12),
            (swapped_a, 16),
            (swapped_b, 24),
            (last_a, 20),
            (last_b, 28),
        ],
    ]
    return sources, small, from_senders


def device_bits():
    group = lax.axis_index("grp")
    device = lax.axis_index("dev")
    return group & 1, group >> 1, device & 1, (device >> 1) & 1, (device >> 2) & 1


def relative_places(place):
    x, y, core, z, far = device_bits()
    mirrored = (place & 25) | ((place & 4) >> 1) | ((place & 2) << 1)
    plain = jnp.where((place & 8) == 0, place, mirrored)
    return plain ^ (core * 16 + far * 8 + x * 4 + y * 2 + z)


def edge_order():
    return relative_places(jnp.arange(CHUNKS, dtype=jnp.int32))


def node_order():
    place = jnp.arange(CHUNKS, dtype=jnp.int32)
    return relative_places(((place & 4) << 2) | ((place & 24) >> 1) | (place & 3))


def shape(*dims, kind=F32):
    return jax.ShapeDtypeStruct(dims, kind)


def params(mebibytes):
    return pltpu.CompilerParams(vmem_limit_bytes=mebibytes << 20)


def whole(*dims):
    return pl.BlockSpec(dims, lambda *_: (0,) * len(dims), pipeline_mode=pl.Buffered(1))


def result(*dims):
    return pl.BlockSpec(dims, lambda *_: (0,) * len(dims))


def per_device(
    node_latent,
    edge_latent,
    node_cotangent,
    edge_cotangent,
    edge_sender,
    edge_receiver,
    live_counts,
    edge_lift,
    edge_bias,
    edge_mix,
    edge_gain,
    node_lift,
    node_bias,
    node_mix,
    node_gain,
):
    width = node_latent.shape[2]
    nodes = node_latent[0]
    count = nodes.shape[0]
    peers = edge_receiver.shape[1]
    slots = edge_receiver.shape[2]
    total_rows = peers * slots
    unit = total_rows * width * width
    edges = edge_latent.reshape(peers, slots, width)
    edge_seed = edge_cotangent.reshape(peers, slots, width)
    receivers = edge_receiver.reshape(peers, slots)
    live = live_counts.reshape(peers)
    mine = lax.axis_index("dev")
    paired = lax.axis_size("dev") == 8 and lax.axis_size("grp") == 4
    packed_rows = count + -(-peers // 16) * 16
    packed_nodes = pl.pallas_call(
        pack_kernel,
        out_shape=shape(packed_rows, width, kind=BF16),
        compiler_params=params(4),
        name="pack",
    )(nodes, edge_sender)
    if paired:
        owners = jnp.arange(peers, dtype=jnp.int32) ^ mine
        edge_places = edge_order()
        node_places = node_order()
        near = swap(packed_nodes, "dev", 2)
        across = swap(packed_nodes, "dev", 4)
        beside, across = lax.optimization_barrier((swap(packed_nodes, "dev", 1), across))
        behind = swap(across, "dev", 2)
        pieces = [packed_nodes, beside]
        pieces = [piece[None] for piece in pieces]
        ranges = [(0, 2), (2, 6), (6, 8)]
    else:
        owners = jnp.arange(peers, dtype=jnp.int32)
        edge_places = node_places = jnp.arange(CHUNKS, dtype=jnp.int32)
        pieces = [lax.all_gather(packed_nodes, "dev")]
        ranges = [(0, peers)]
    gathered_rows = pieces[0].shape[1]

    anywhere = pl.BlockSpec(memory_space=pl.ANY)
    bias_row = edge_bias.reshape(1, width)
    gain_row = edge_gain.reshape(1, width)

    owned = pl.BlockSpec((1, slots, width), lambda i: (i, 0, 0))
    pre = pl.pallas_call(
        lift_kernel,
        grid=(peers,),
        in_specs=[
            owned,
            whole(peers, slots),
            whole(count, width),
            whole(3 * width, width),
            whole(1, width),
        ],
        out_specs=owned,
        out_shape=shape(peers, slots, width),
        compiler_params=params(12),
        cost_estimate=pl.CostEstimate(
            flops=5 * unit, bytes_accessed=6 * total_rows * width, transcendentals=0
        ),
        name="lift",
    )(edges, receivers, nodes, edge_lift, bias_row)

    def by_owner(*dims):
        return pl.BlockSpec(
            (1,) + dims, lambda i, owner, *_: (owner[i],) + (0,) * len(dims)
        )

    group = 2

    def grouped(*dims):
        return pl.BlockSpec((group,) + dims, lambda i, *_: (i,) + (0,) * len(dims))

    saved = []
    summed = None
    for begin, end in ranges:
        first, last = begin == 0, end == peers
        if last and not first:
            behind, summed = lax.optimization_barrier((behind, summed))
        if not first:
            for piece in [behind] if last else [near, across]:
                pieces += [piece[None], swap(piece, "dev", 1)[None]]
        chosen = pieces[begin:] if paired else pieces

        operands = chosen + [
            pre,
            receivers,
            nodes,
            edge_lift,
            edge_mix,
            gain_row,
        ]
        in_specs = [anywhere] * len(chosen) + [
            by_owner(slots, width),
            whole(peers, slots),
            whole(count, width),
            pl.BlockSpec((width, width), lambda *_: (1, 0), pipeline_mode=pl.Buffered(1)),
            whole(width, width),
            whole(1, width),
        ]
        aliases = {}
        if not first:
            aliases = {4 + len(operands) + j: j for j in range(4)}
            operands += saved + [summed]
            in_specs += [anywhere] * 4 + [whole(count, width)]
        out_specs = [by_owner(slots, width)] * 3 + [by_owner(slots, 1)]
        out_shape = [shape(peers, slots, width, kind=BF16)] * 3 + [shape(peers, slots, 1)]
        scratch = [
            pltpu.VMEM((end - begin, gathered_rows, width), BF16),
            pltpu.SemaphoreType.DMA((len(chosen),)),
        ]
        if last:
            operands += [
                node_cotangent[0],
                node_lift,
                node_bias.reshape(1, width),
                node_mix,
                node_gain.reshape(1, width),
            ]
            in_specs += [whole(count, width), anywhere, whole(1, width), anywhere, whole(1, width)]
            out_specs += [
                result(count, width),
                result(count, width),
                result(3 * width, width),
                result(2, width),
            ]
            out_shape += [
                shape(count, width),
                shape(count, width, kind=BF16),
                shape(3 * width, width, kind=BF16),
                shape(2, width),
            ]
            scratch += [
                pltpu.VMEM((count, width), F32),
                pltpu.VMEM((3 * width, width), F32),
                pltpu.VMEM((2 * width, width), BF16),
                pltpu.VMEM((width, width), BF16),
                pltpu.SemaphoreType.DMA((2,)),
            ]
        else:
            out_specs.append(result(count, width))
            out_shape.append(shape(count, width))
        results = pl.pallas_call(
            functools.partial(forward_kernel, len(chosen), first, last),
            grid_spec=pltpu.PrefetchScalarGridSpec(
                num_scalar_prefetch=4,
                grid=(end - begin,),
                in_specs=in_specs,
                out_specs=out_specs,
                scratch_shapes=scratch,
            ),
            out_shape=out_shape,
            input_output_aliases=aliases,
            compiler_params=params(24),
            cost_estimate=pl.CostEstimate(
                flops=4 * unit,
                bytes_accessed=8 * total_rows * width,
                transcendentals=total_rows * width,
            ),
            name="forward_%d" % begin,
        )(owners[begin:end], live, node_places, mine.reshape(1), *operands)
        saved = list(results[:4])
        if last:
            base, summed_grad, node_packed, node_small = results[4:]
        else:
            summed = results[4]
    hidden, normed, slope, inverse = saved

    if paired:
        node_kept, node_got = node_start(node_packed)
    grad_edges, partial, grad_nodes, edge_packed, edge_small = pl.pallas_call(
        functools.partial(backward_kernel, len(pieces)),
        grid_spec=pltpu.PrefetchScalarGridSpec(
            num_scalar_prefetch=4,
            grid=(peers // group,),
            in_specs=[anywhere] * len(pieces)
            + [
                grouped(slots, width),
                grouped(slots, width),
                whole(peers, slots),
                grouped(slots, width),
                grouped(slots, width),
                grouped(slots, width),
                grouped(slots, 1),
                whole(count, width),
                whole(count, width),
                whole(count, width),
                whole(3 * width, width),
                whole(width, width),
                whole(1, width),
            ],
            out_specs=[
                grouped(slots, width),
                pl.BlockSpec(
                    (2, group // 2, count, width),
                    lambda i, arrival, *_: (0, arrival[i * group] // group, 0, 0),
                ),
                result(count, width),
                result(4 * width, width),
                result(2, width),
            ],
            scratch_shapes=[
                pltpu.VMEM((count, width), F32),
                pltpu.VMEM((4 * width, width), F32),
                pltpu.VMEM((peers, gathered_rows, width), BF16),
                pltpu.VMEM((group * slots, width), BF16),
                pltpu.VMEM((group * slots, width), BF16),
                pltpu.VMEM((group, count, width), BF16),
                pltpu.SemaphoreType.DMA((len(pieces),)),
            ],
        ),
        out_shape=[
            shape(peers, slots, width, kind=BF16),
            shape(2, peers // 2, count, width, kind=BF16),
            shape(count, width),
            shape(4 * width, width, kind=BF16),
            shape(2, width),
        ],
        compiler_params=params(30),
        cost_estimate=pl.CostEstimate(
            flops=14 * unit, bytes_accessed=20 * total_rows * width, transcendentals=0
        ),
        name="backward",
    )(
        owners,
        live,
        edge_places,
        mine.reshape(1),
        *pieces,
        edges,
        edge_seed,
        receivers,
        hidden,
        normed,
        slope,
        inverse,
        nodes,
        base,
        summed_grad,
        edge_lift,
        edge_mix,
        gain_row,
    )

    if paired:
        edge_packed, edge_small, *node_got = lax.optimization_barrier(
            (edge_packed, edge_small, *node_got)
        )
    small = jnp.concatenate([edge_small, node_small])
    if paired:
        sources, small, from_senders = reduce_all(
            edge_packed, node_kept, node_got, partial, small
        )
    else:
        node_sum, edge_sum, small = lax.psum(
            (node_packed.astype(F32), edge_packed.astype(F32), small), ("grp", "dev")
        )
        interleaved = jnp.concatenate(
            [
                edge_sum.reshape(CHUNKS, 4 * width // CHUNKS, width),
                node_sum.reshape(CHUNKS, 3 * width // CHUNKS, width),
            ],
            axis=1,
        )
        sources = [[(interleaved.reshape(7 * width, width).astype(BF16), 0)]]
        ordered = jnp.swapaxes(partial, 0, 1).reshape(peers, count, width)
        from_senders = lax.psum_scatter(ordered.astype(F32), "dev", scatter_dimension=0)
    grad_nodes = grad_nodes + contract_features(
        from_senders.astype(BF16), edge_lift[width : 2 * width]
    )
    groups = lax.axis_size("grp") * lax.axis_size("dev")
    edge_scale = float(total_rows * groups) ** (-0.5)
    node_scale = float(count * groups) ** (-0.5)
    totals = [3 * width, width, 2 * width, width]
    unpacked = []
    for part in sources:
        part, starts = zip(*part)
        places = sum(source.shape[0] for source in part) * CHUNKS // (7 * width)
        unpacked = pl.pallas_call(
            functools.partial(unpack_kernel, (edge_scale, node_scale), starts),
            grid_spec=pltpu.PrefetchScalarGridSpec(
                num_scalar_prefetch=1,
                grid=(1,),
                in_specs=[whole(*source.shape) for source in part] + [anywhere] * len(unpacked),
                out_specs=[anywhere] * 4,
                scratch_shapes=[
                    pltpu.VMEM((places * total // CHUNKS, width), F32) for total in totals
                ]
                + [pltpu.SemaphoreType.DMA((4, places))],
            ),
            out_shape=[shape(total, width) for total in totals],
            input_output_aliases={1 + len(part) + j: j for j in range(len(unpacked))},
            compiler_params=params(20),
            cost_estimate=pl.CostEstimate(
                flops=0, bytes_accessed=42 * places * width * width // CHUNKS, transcendentals=0
            ),
            name="unpack_%d" % starts[0],
        )(edge_places, *part, *unpacked)
    edge_lift_grad, edge_mix_grad, node_lift_grad, node_mix_grad = unpacked
    return (
        grad_nodes[None],
        grad_edges.reshape(1, 1, peers, slots, width),
        edge_lift_grad,
        small[0] * edge_scale,
        edge_mix_grad,
        small[1] * edge_scale,
        node_lift_grad,
        small[2] * node_scale,
        node_mix_grad,
        small[3] * node_scale,
    )


def solution(mesh):
    return jax.shard_map(
        per_device,
        mesh=mesh,
        in_specs=(
            P("grp", "dev", None),
            P("grp", "dev", None, None, None),
            P("grp", "dev", None),
            P("grp", "dev", None, None, None),
            P(None, "dev", None),
            P("dev", None, None),
            P("dev", None),
            P(),
            P(),
            P(),
            P(),
            P(),
            P(),
            P(),
            P(),
        ),
        out_specs=(
            P("grp", "dev", None),
            P("grp", "dev", None, None, None),
            P(),
            P(),
            P(),
            P(),
            P(),
            P(),
            P(),
            P(),
        ),
        check_vma=False,
    )
```
